512 devices in a mesh: leaf: 128 (over z, y, core), vec: 4 (over x).
Axes of the slice: x: 4, y: 8, z: 8, core: 2. Of those that a mesh axis runs over, the one named last changes fastest.
Arguments:
- vectors: bfloat16 [16, 1048576], P('vec', 'leaf'), may hold values from -6 to 6
- near_blocks: bfloat16 [4096, 2, 256, 256], P(('leaf', 'vec')), may hold values from -0.25 to 0.25
- near_list: int32 [4096, 2], P(('leaf', 'vec')), may hold values from 0 to 4095, as said below
- bases: bfloat16 [4096, 256, 64], P(('leaf', 'vec')), may hold values from -0.375 to 0.375
- leaf_maps: bfloat16 [4096, 64, 64], P('leaf'), may hold values from -0.25 to 0.25
- far_blocks: bfloat16 [4096, 6, 64, 64], P('leaf'), may hold values from -0.4375 to 0.4375
- far_list: int32 [4096, 6], P('leaf'), may hold values from 0 to 4095, as said below
- far_count: int32 [4096], P('leaf'), may hold values from 1 to 6, as said below
- level_maps: bfloat16 [128, 7, 64, 64], P('leaf'), may hold values from -0.75 to 0.75
- ancestor_coupling_blocks: bfloat16 [128, 7, 64, 64], P('leaf'), may hold values from -0.25 to 0.25
Outputs:
- product: float32 [16, 1048576], P('vec', 'leaf')
The draws below stay inside these ranges and needn't reach their ends.
Inputs may be any that keep to these rules, and one draw needn't show every extreme that they name: Both column clusters of a leaf's near-field blocks lie in the leaf's own subtree: near_list[l, n] // 32 == l // 32. Every coupling partner lies in the leaf's own subtree or in the subtree just before or after it: far_list[l, f] // 32 differs from l // 32 by at most one. Slots at or beyond far_count are present but unused. `far_count`: used coupling slots of each leaf; some leaf uses all 6.
All inputs are finite; a program needn't handle non-finite values.
Results may differ from the reference program's by a relative error of at most 0.0055.
Values may be sent and summed in bfloat16 or wider, within the bound.
A program may use at most 64 MiB of HBM per device.

```python
import jax
import jax.numpy as jnp
from jax import lax

CLUSTER = 256
RANK = 64
VECTORS = 16
NNEAR = 2
NFAR = 6
LEAVES_DEV = 32
NLEAF = 4096
POINTS = 1048576
TOPS = 7
N_LEAF = 128


def draw_near_list(key, part):
    key = jax.random.fold_in(key, 11)
    leaf_ids = jnp.arange(NLEAF)
    starts = leaf_ids // LEAVES_DEV * LEAVES_DEV
    chosen = starts[:, None] + jax.random.randint(key, (NLEAF, NNEAR), 0, LEAVES_DEV)
    chosen = chosen.at[0, 0].set(0).at[NLEAF - 1, 0].set(NLEAF - 1)
    return chosen.astype(jnp.int32)


def draw_far_list(key, part):
    key = jax.random.fold_in(key, 23)
    leaf_ids = jnp.arange(NLEAF)
    starts = leaf_ids // LEAVES_DEV * LEAVES_DEV
    chosen = starts[:, None] + jax.random.randint(key, (NLEAF, NFAR), -LEAVES_DEV, 2 * LEAVES_DEV)
    chosen = jnp.clip(chosen, 0, NLEAF - 1)
    chosen = chosen.at[0, 0].set(0).at[NLEAF - 1, 0].set(NLEAF - 1)
    return chosen.astype(jnp.int32)


def draw_far_count(key, part):
    key = jax.random.fold_in(key, 37)
    key_cap, key_cnt, key_pos = jax.random.split(key, 3)
    caps = jax.random.randint(key_cap, (NLEAF // LEAVES_DEV,), NFAR // 2, NFAR + 1)
    cap_leaf = jnp.repeat(caps, LEAVES_DEV)
    counts = 1 + jax.random.randint(key_cnt, (NLEAF,), 0, NFAR) % cap_leaf
    place = jax.random.randint(key_pos, (), 0, NLEAF)
    counts = jnp.where(jnp.arange(NLEAF) == place, NFAR, counts)
    return counts.astype(jnp.int32)


def levels(key, dims, cuts, least, top_value):
    def one(dim, parts):
        steps = jax.random.uniform(jax.random.fold_in(jax.random.fold_in(key, 6), dim), (parts,), jnp.float32, least / len(cuts), top_value / len(cuts))
        return jnp.repeat(jnp.exp(steps), dims[dim] // parts).reshape((-1,) + (1,) * (len(dims) - dim - 1))

    level = one(*cuts[0])
    for cut in cuts[1:]:
        level = level * one(*cut)
    return level


def bell_draw(key, shape, deviation, bound, cuts=(), kind=jnp.bfloat16):
    entries = jax.random.normal(key, shape, jnp.float32) * deviation
    if len(cuts) > 0:
        entries = levels(key, shape, cuts, -0.22, 0.18) * entries
    return jnp.clip(entries, min=-bound, max=bound).astype(kind)


def setup_inputs(seed: int = 0) -> dict:
    streams_of = jax.random.split(jax.random.key(seed), 11)
    return {
        "vectors": bell_draw(streams_of[0], (VECTORS, POINTS), 1.0, 6.0, ((0, 4), (1, 128))),
        "near_blocks": bell_draw(streams_of[1], (NLEAF, NNEAR, CLUSTER, CLUSTER), (CLUSTER * NNEAR) ** -0.5, 0.25, ((0, 512),)),
        "near_list": draw_near_list(jax.random.fold_in(streams_of[10], 71), 0),
        "bases": bell_draw(streams_of[3], (NLEAF, CLUSTER, RANK), CLUSTER ** -0.5, 0.375, ((0, 512),)),
        "leaf_maps": bell_draw(streams_of[4], (NLEAF, RANK, RANK), (RANK * 8) ** -0.5, 0.25, ((0, 128),)),
        "far_blocks": bell_draw(streams_of[5], (NLEAF, NFAR, RANK, RANK), (RANK * 3) ** -0.5, 0.4375, ((0, 128),)),
        "far_list": draw_far_list(jax.random.fold_in(streams_of[10], 71), 0),
        "far_count": draw_far_count(jax.random.fold_in(streams_of[10], 71), 0),
        "level_maps": bell_draw(streams_of[8], (N_LEAF, TOPS, RANK, RANK), RANK ** -0.5, 0.75, ((0, 128),)),
        "ancestor_coupling_blocks": bell_draw(streams_of[9], (N_LEAF, TOPS, RANK, RANK), (RANK * TOPS) ** -0.5, 0.25, ((0, 128),)),
    }


def reference(vectors, near_blocks, near_list, bases, leaf_maps, far_blocks, far_list, far_count, level_maps, ancestor_coupling_blocks):
    subtrees = NLEAF // LEAVES_DEV
    split_x = vectors.reshape(VECTORS, NLEAF, CLUSTER)
    by_tree = split_x.reshape(VECTORS, subtrees, LEAVES_DEV, CLUSTER).transpose(1, 0, 2, 3)

    def near_one(packed):
        input_hierarchy, blocks, lists, offset = packed
        picked = input_hierarchy[:, lists - offset]
        return jnp.einsum("qnab,vqnb->vqa", blocks.astype(jnp.float32), picked.astype(jnp.float32))

    offsets = (jnp.arange(subtrees) * LEAVES_DEV).astype(jnp.int32)
    near_field = lax.map(near_one, (by_tree, near_blocks.reshape(subtrees, LEAVES_DEV, NNEAR, CLUSTER, CLUSTER),
                                    near_list.reshape(subtrees, LEAVES_DEV, NNEAR), offsets))
    bases_tree = bases.reshape(subtrees, LEAVES_DEV, CLUSTER, RANK)

    def coeff_one(packed):
        input_hierarchy, basis_factor = packed
        return jnp.einsum("yot,nyo->ynt", basis_factor.astype(jnp.float32), input_hierarchy.astype(jnp.float32)).astype(jnp.bfloat16)

    coeffs = lax.map(coeff_one, (by_tree, bases_tree)).reshape(NLEAF, VECTORS, RANK)
    live_slot = (jnp.arange(NFAR)[None, :] < far_count[:, None])
    picked = coeffs[far_list]
    masked = jnp.where(live_slot[:, :, None, None], picked, jnp.zeros_like(picked))

    def far_one(packed):
        blocks, coefs = packed
        return jnp.einsum("lfab,lfvb->lva", blocks.astype(jnp.float32), coefs.astype(jnp.float32))

    distant_interaction = lax.map(far_one, (far_blocks.reshape(subtrees, LEAVES_DEV, NFAR, RANK, RANK),
                                  masked.reshape(subtrees, LEAVES_DEV, NFAR, VECTORS, RANK)))
    maps_tree = leaf_maps.reshape(subtrees, LEAVES_DEV, RANK, RANK).astype(jnp.float32)
    root_coef = jnp.einsum("slkj,slvk->svj", maps_tree,
                           coeffs.reshape(subtrees, LEAVES_DEV, VECTORS, RANK).astype(jnp.float32)).astype(jnp.bfloat16)
    scales = 2.0 ** (-0.5 * jnp.arange(TOPS, dtype=jnp.float32))
    stacked = jnp.einsum("stkj,svk->stvj", level_maps.astype(jnp.float32), root_coef.astype(jnp.float32)) * scales[None, :, None, None]
    tree_ids = jnp.arange(subtrees)
    siblings = []
    for level in range(TOPS):
        sums = stacked[:, level].reshape(subtrees >> level, 2 ** level, VECTORS, RANK).sum(axis=1)
        siblings.append(sums[(tree_ids >> level) ^ 1])
    sib_bf = jnp.stack(siblings, axis=1).astype(jnp.bfloat16)
    coupled_up = jnp.einsum("stkj,stvj->svk", ancestor_coupling_blocks.astype(jnp.float32), sib_bf.astype(jnp.float32)).astype(jnp.bfloat16)
    leaf_output_rows = (distant_interaction + jnp.einsum("slkj,svj->slvk", maps_tree, coupled_up.astype(jnp.float32))).astype(jnp.bfloat16)
    distant_contribution = jnp.einsum("slck,slvk->svlc", bases_tree.astype(jnp.float32), leaf_output_rows.astype(jnp.float32))
    total = near_field + distant_contribution
    return total.transpose(1, 0, 2, 3).reshape(VECTORS, POINTS)
```

```python
import functools

import jax
import jax.numpy as jnp
from jax import lax
from jax.experimental import pallas as pl
from jax.experimental.pallas import tpu as pltpu
from jax.sharding import PartitionSpec as P

MESH = pl.DeviceIdType.MESH
F32 = jnp.float32
BF16 = jnp.bfloat16
NN = (((1,), (0,)), ((), ()))
NT = (((1,), (1,)), ((), ()))


def dot(a, b, dims=NN):
    return lax.dot_general(a, b, dims, preferred_element_type=F32)


def drain(ref, sem):
    pltpu.make_async_copy(ref, ref, sem).wait()


def flipped(value, mask, bits):
    out = 0
    for b in range(bits):
        bit = lax.rem(value // (1 << b), 2)
        out = out + (1 << b) * ((1 - bit) if (mask >> b) & 1 else bit)
    return out


def kernel(
    ny,
    nz,
    vectors,
    near_blocks,
    near_list,
    bases,
    leaf_maps,
    far_blocks,
    far_list,
    far_count,
    level_maps,
    coupling,
    out,
    xs,
    x16,
    near_b,
    near_l,
    basis,
    maps,
    far_b,
    far_l,
    far_c,
    level_own,
    level_sib,
    coup,
    roots,
    coefs,
    weights,
    terms,
    tree,
    near_out,
    far_out,
    result,
    loc,
    send,
    recv,
    tree_recv,
    token,
):
    leaf = lax.axis_index("leaf")
    q = lax.axis_index("vec")
    nx = 4
    core = lax.rem(leaf, 2)
    chip = leaf // 2
    y = lax.rem(chip, ny)
    z = chip // ny
    ybits, zbits = ny.bit_length() - 1, nz.bit_length() - 1
    levels = 1 + ybits + zbits

    def leaf_at(zz, yy, cc):
        return (zz * ny + yy) * 2 + cc

    copies = []

    def load(src, dst):
        c = pltpu.make_async_copy(src, dst, loc.at[len(copies)])
        c.start()
        copies.append(c)
        return c

    for g in range(4):
        pltpu.make_async_copy(
            vectors.at[:, pl.ds(g * 2048, 2048)], xs.at[q * 4 + g], loc.at[15]
        ).start()
    l_basis = load(bases, basis)
    l_maps = load(leaf_maps.at[pl.ds(q * 8, 8)], maps)
    l_level = load(level_maps.at[0], level_own)
    l_nl = load(near_list, near_l)
    l_fl = load(far_list, far_l)
    l_fc = load(far_count, far_c)
    l_coup = load(coupling.at[0], coup)
    l_near = load(near_blocks, near_b)
    l_far = load(far_blocks.at[pl.ds(q * 8, 8)], far_b)

    x_peers = [lax.rem(q + d, nx) for d in (1, 2, 3)]
    y_peers = [flipped(y, d, ybits) for d in range(1, ny)]
    z_peers = [flipped(z, d, zbits) for d in range(1, nz)]
    up = lax.rem(leaf + 1, 2 * ny * nz)
    down = lax.rem(leaf + 2 * ny * nz - 1, 2 * ny * nz)
    off_chip = jnp.where(core == 1, up, down)
    sib = leaf_at(z, y, 1 - core)

    near_by = [(leaf, p) for p in x_peers]
    near_by += [(sib, lax.rem(q + d, nx)) for d in range(4)]
    in_plane = [(leaf_at(z, yy, core), q) for yy in y_peers]
    in_plane += [(leaf_at(zz, y, core), q) for zz in z_peers]
    beside = [(off_chip, lax.rem(q + d, nx)) for d in range(4)]

    barrier = pltpu.get_barrier_semaphore()
    first = near_by + in_plane + beside
    for dev in first:
        pl.semaphore_signal(barrier, inc=1, device_id=dev, device_id_type=MESH)
    drain(xs.at[pl.ds(0, 4)], loc.at[15])
    pl.semaphore_wait(barrier, len(first))

    def push(src, dst, k, dev, rsem=None):
        pltpu.make_async_remote_copy(
            src_ref=src,
            dst_ref=dst,
            send_sem=send.at[k],
            recv_sem=recv.at[k] if rsem is None else rsem,
            device_id=dev,
            device_id_type=MESH,
        ).start()

    for p in x_peers:
        push(xs.at[q * 4 + p], xs.at[q * 4 + p], 0, (leaf, p))
    push(level_maps.at[0], level_sib, 1, (sib, q))
    for d in (1, 2, 3):
        for p in x_peers:
            g = lax.rem(p + d, nx)
            push(xs.at[q * 4 + g], xs.at[q * 4 + g], 2, (leaf, p))
    for yy in y_peers:
        pl.semaphore_signal(
            token, inc=1, device_id=(leaf_at(z, yy, core), q), device_id_type=MESH
        )

    def block(g):
        parts = [xs[s * 4 + g].astype(F32) for s in range(4)]
        return jnp.concatenate(parts, axis=0).astype(BF16)

    l_basis.wait()
    l_maps.wait()
    drain(xs.at[pl.ds(0, 3)], recv.at[0])
    own = block(q)
    pairs = []
    for i in range(4):
        two = [
            dot(own[:, (2 * i + j) * 256 : (2 * i + j + 1) * 256], basis[2 * i + j], NT)
            for j in range(2)
        ]
        pairs.append(jnp.concatenate(two, axis=1).astype(BF16))
    part = dot(jnp.concatenate(pairs, axis=1), maps[...].reshape(512, 64))
    roots[q] = part
    for dev in near_by[:3]:
        push(roots.at[q], roots.at[q], 3, dev)
    for dev in near_by[3:]:
        push(roots.at[q], roots.at[4 + q], 3, dev)
    mine = 16 + q * 4
    for i in range(4):
        coefs[mine + i] = pairs[i]
    src = coefs.at[pl.ds(mine, 4)]
    for dev in near_by[:3]:
        push(src, src, 4, dev)
    for d in range(4):
        p = lax.rem(q + d, nx)
        push(src, coefs.at[pl.ds(q * 4, 4)], 4, (up, p))
        push(src, coefs.at[pl.ds(32 + q * 4, 4)], 4, (down, p))

    l_level.wait()
    drain(level_sib, recv.at[1])
    for half, lev in ((0, level_own), (1, level_sib)):
        for i in range(levels // 2):
            t = 1 + 2 * i
            ls = [lev[t]] + ([lev[t + 1]] if t + 1 < levels else [lev[t]])
            weights[half * 64 : half * 64 + 64, i * 128 : i * 128 + 128] = jnp.concatenate(
                ls, axis=1
            )
    drain(xs.at[pl.ds(0, 9)], recv.at[2])
    for g in range(4):
        group = block(g)
        for i in range(8):
            x16[g * 8 + i] = group[:, i * 256 : (i + 1) * 256]

    drain(roots.at[pl.ds(0, 7)], recv.at[3])
    root_own = (roots[0] + roots[1]) + (roots[2] + roots[3])
    root_sib = (roots[4] + roots[5]) + (roots[6] + roots[7])
    root_sib = root_sib.astype(BF16)
    both = jnp.concatenate([root_own.astype(BF16), root_sib], axis=1)
    sums = dot(both, weights[...])
    for t in range(1, levels):
        term = sums[:, (t - 1) * 64 : t * 64] * (2.0 ** (-0.5 * t))
        terms[t - 1] = jnp.concatenate([term[0:8], term[8:16]], axis=1).astype(BF16)
    if ny > 1:
        pl.semaphore_wait(token, ny - 1)
    for d in range(ny * nz - 1, 0, -1):
        t = d.bit_length()
        zz = flipped(z, d // ny, zbits)
        yy = flipped(y, d % ny, ybits)
        push(
            terms.at[t - 1], tree.at[d], 5, (leaf_at(zz, yy, core), q), tree_recv.at[t - 1]
        )

    l_coup.wait()
    level0 = dot(root_sib, level_sib[0])
    coupled = dot(level0.astype(BF16), coup[0], NT)
    l_nl.wait()
    l_near.wait()
    for i in range(8):
        total = None
        for n in range(2):
            at = jnp.clip(near_l[n, i] - leaf * 32, 0, 31)
            one = dot(x16[at], near_b[i, n], NT)
            total = one if total is None else total + one
        near_out[:, i * 256 : (i + 1) * 256] = total
    l_fl.wait()
    l_fc.wait()
    l_far.wait()
    drain(coefs.at[pl.ds(0, 44)], recv.at[4])
    for i in range(8):
        total = None
        for f in range(6):
            at = jnp.clip(far_l[f, q * 8 + i] - leaf * 32 + 32, 0, 95)
            pair = coefs[at // 2].astype(F32)
            odd = jnp.full((16, 64), lax.rem(at, 2), jnp.int32) == 1
            used = jnp.full((16, 64), far_c[q * 8 + i], jnp.int32) > f
            value = jnp.where(odd, pair[:, 64:], pair[:, :64])
            value = jnp.where(used, value, 0.0).astype(BF16)
            one = dot(value, far_b[i, f], NT)
            total = one if total is None else total + one
        far_out[:, i * 64 : (i + 1) * 64] = total

    for t in range(1, levels):
        lo, hi = 1 << (t - 1), 1 << t
        drain(tree.at[pl.ds(lo, hi - lo)], tree_recv.at[t - 1])
        acc = tree[lo].astype(F32)
        for d in range(lo + 1, hi):
            acc = acc + tree[d].astype(F32)
        sibling = jnp.concatenate([acc[:, :64], acc[:, 64:]], axis=0).astype(BF16)
        coupled = coupled + dot(sibling, coup[t], NT)
    lifted = dot(coupled.astype(BF16), maps[...].reshape(512, 64), NT)
    leaf_out = (far_out[...] + lifted).astype(BF16)
    for i in range(8):
        far = dot(leaf_out[:, i * 64 : (i + 1) * 64], basis[i])
        total = far + near_out[:, i * 256 : (i + 1) * 256]
        for p in range(4):
            result[p, :, i * 256 : (i + 1) * 256] = total[4 * p : 4 * p + 4].astype(BF16)
    for p in x_peers:
        push(result.at[p], out.at[q], 6, (leaf, p))
    last = pltpu.make_async_copy(result.at[q], out.at[q], loc.at[14])
    last.start()
    last.wait()
    drain(result.at[pl.ds(0, 3)], recv.at[6])
    drain(xs.at[pl.ds(0, 3)], send.at[0])
    drain(level_sib, send.at[1])
    drain(xs.at[pl.ds(0, 9)], send.at[2])
    drain(roots.at[pl.ds(0, 7)], send.at[3])
    drain(coefs.at[pl.ds(0, 44)], send.at[4])
    drain(tree.at[pl.ds(1, ny * nz - 1)], send.at[5])
    drain(result.at[pl.ds(0, 3)], send.at[6])


def local(
    ny,
    nz,
    vectors,
    near_blocks,
    near_list,
    bases,
    leaf_maps,
    far_blocks,
    far_list,
    far_count,
    level_maps,
    coupling,
):
    levels = level_maps.shape[1]
    anywhere = pl.BlockSpec(memory_space=pl.ANY)
    wide = 128 * (levels // 2)
    gathered = pl.pallas_call(
        functools.partial(kernel, ny, nz),
        out_shape=jax.ShapeDtypeStruct((4, 4, 2048), BF16),
        in_specs=[pl.BlockSpec(memory_space=pltpu.HBM)] * 10,
        out_specs=anywhere,
        scratch_shapes=[
            pltpu.VMEM((16, 4, 2048), BF16),
            pltpu.VMEM((32, 16, 256), BF16),
            pltpu.VMEM((8, 2, 256, 256), BF16),
            pltpu.SMEM((2, 8), jnp.int32),
            pltpu.VMEM((8, 64, 256), BF16),
            pltpu.VMEM((8, 64, 64), BF16),
            pltpu.VMEM((8, 6, 64, 64), BF16),
            pltpu.SMEM((6, 32), jnp.int32),
            pltpu.SMEM((32,), jnp.int32),
            pltpu.VMEM((levels, 64, 64), BF16),
            pltpu.VMEM((levels, 64, 64), BF16),
            pltpu.VMEM((levels, 64, 64), BF16),
            pltpu.VMEM((8, 16, 64), F32),
            pltpu.VMEM((48, 16, 128), BF16),
            pltpu.VMEM((128, wide), BF16),
            pltpu.VMEM((levels - 1, 8, 128), BF16),
            pltpu.VMEM((ny * nz, 8, 128), BF16),
            pltpu.VMEM((16, 2048), F32),
            pltpu.VMEM((16, 512), F32),
            pltpu.VMEM((4, 4, 2048), BF16),
            pltpu.SemaphoreType.DMA((16,)),
            pltpu.SemaphoreType.DMA((7,)),
            pltpu.SemaphoreType.DMA((7,)),
            pltpu.SemaphoreType.DMA((levels - 1,)),
            pltpu.SemaphoreType.REGULAR,
        ],
        compiler_params=pltpu.CompilerParams(
            collective_id=0, has_side_effects=True, vmem_limit_bytes=64 * 2**20
        ),
        name="h2_product",
    )(
        vectors,
        near_blocks,
        near_list.T,
        bases.transpose(0, 2, 1),
        leaf_maps,
        far_blocks,
        far_list.T,
        far_count,
        level_maps,
        coupling,
    )
    return gathered.astype(F32).transpose(1, 0, 2).reshape(4, 8192)


def solution(mesh):
    leaves = mesh.shape["leaf"]
    ny = 8 if leaves == 128 else 2
    nz = leaves // (2 * ny)
    in_specs = (
        P("vec", "leaf"),
        P(("leaf", "vec"), None, None, None),
        P(("leaf", "vec"), None),
        P(("leaf", "vec"), None, None),
        P("leaf", None, None),
        P("leaf", None, None, None),
        P("leaf", None),
        P("leaf"),
        P("leaf", None, None, None),
        P("leaf", None, None, None),
    )
    return jax.shard_map(
        functools.partial(local, ny, nz),
        mesh=mesh,
        in_specs=in_specs,
        out_specs=P("vec", "leaf"),
        check_vma=False,
    )
```

```python
import functools

import jax
import jax.numpy as jnp
from jax import lax
from jax.experimental import pallas as pl
from jax.experimental.pallas import tpu as pltpu
from jax.sharding import PartitionSpec as P

MESH = pl.DeviceIdType.MESH
F32 = jnp.float32
BF16 = jnp.bfloat16
NN = (((1,), (0,)), ((), ()))
NT = (((1,), (1,)), ((), ()))
TN = (((0,), (0,)), ((), ()))
NX, NY, NZ = 4, 8, 8
LEVELS = 7


def dot(a, b, dims=NN):
    return lax.dot_general(a, b, dims, preferred_element_type=F32)


def drain(ref, sem):
    pltpu.make_async_copy(ref, ref, sem).wait()


def flipped(value, mask):
    out = 0
    for b in range(3):
        bit = lax.rem(value // (1 << b), 2)
        out = out + (1 << b) * ((1 - bit) if (mask >> b) & 1 else bit)
    return out


def twice(block):
    zero = jnp.zeros_like(block)
    return jnp.concatenate(
        [jnp.concatenate([block, zero], axis=1), jnp.concatenate([zero, block], axis=1)],
        axis=0,
    )


REACH = (0, 1, 2, 3, 4, 3, 2, 3)
FARTHEST_FIRST = sorted(range(1, NY * NZ), key=lambda d: -(REACH[d // NY] + REACH[d % NY]))


def kernel(
    vectors,
    near_blocks,
    near_list,
    bases,
    leaf_maps,
    far_blocks,
    far_list,
    far_count,
    level_maps,
    coupling,
    out,
    xs,
    own_x,
    x16,
    near_b,
    near_l,
    basis,
    maps,
    far_b,
    far_l,
    far_c,
    level_own,
    level_sib,
    coup,
    lift,
    weights,
    pair_coup,
    roots,
    coefs,
    terms,
    tree,
    local_out,
    result,
    loc,
    send,
    recv,
    tree_recv,
    token,
):
    leaf = lax.axis_index("leaf")
    q = lax.axis_index("vec")
    core = lax.rem(leaf, 2)
    chip = leaf // 2
    y = lax.rem(chip, NY)
    z = chip // NY

    def leaf_at(zz, yy, cc):
        return (zz * NY + yy) * 2 + cc

    sib = leaf_at(z, y, 1 - core)
    up = lax.rem(leaf + 1, 2 * NY * NZ)
    down = lax.rem(leaf + 2 * NY * NZ - 1, 2 * NY * NZ)
    x_peers = [lax.rem(q + d, NX) for d in (1, 2, 3)]
    by_root = [(leaf, p) for p in x_peers] + [(sib, lax.rem(q + d, NX)) for d in range(4)]
    steps = (1, 2, NY - 2, NY - 1)
    close = [(leaf_at(z, lax.rem(y + d, NY), core), q) for d in steps]
    close += [(leaf_at(lax.rem(z + d, NZ), y, core), q) for d in steps]
    row = [(leaf_at(z, lax.rem(y + d, NY), core), q) for d in range(1, NY)]

    barrier = pltpu.get_barrier_semaphore()
    for dev in by_root + close:
        pl.semaphore_signal(barrier, inc=1, device_id=dev, device_id_type=MESH)

    copies = []

    def load(src, dst):
        c = pltpu.make_async_copy(src, dst, loc.at[len(copies)])
        c.start()
        copies.append(c)
        return c

    l_basis = load(bases, basis)
    l_maps = load(leaf_maps.at[pl.ds(q * 8, 8)], maps)
    for g in range(4):
        pltpu.make_async_copy(
            vectors.at[:, pl.ds(g * 2048, 2048)], xs.at[q * 4 + g], loc.at[15]
        ).start()
    l_level = load(level_maps.at[0], level_own)
    l_coup = load(coupling.at[0], coup)
    l_nl = load(near_list, near_l)
    l_fl = load(far_list, far_l)
    l_fc = load(far_count, far_c)
    l_near = load(near_blocks, near_b)
    l_far = load(far_blocks.at[pl.ds(q * 8, 8)], far_b)

    pl.semaphore_wait(barrier, len(by_root + close))

    def push(src, dst, k, dev, rsem=None):
        pltpu.make_async_remote_copy(
            src_ref=src,
            dst_ref=dst,
            send_sem=send.at[k],
            recv_sem=recv.at[k] if rsem is None else rsem,
            device_id=dev,
            device_id_type=MESH,
        ).start()

    def chunk(g):
        return vectors.at[:, pl.ds(pl.multiple_of(g * 2048, 2048), 2048)]

    for p in x_peers:
        push(chunk(p), xs.at[q * 4 + p], 0, (leaf, p))
    push(level_maps.at[0], level_sib, 1, (sib, q))
    for dev in close:
        pl.semaphore_signal(token.at[0], inc=1, device_id=dev, device_id_type=MESH)

    l_basis.wait()
    l_maps.wait()
    for i in range(8):
        block = dot(maps[i], basis[i], TN).astype(BF16)
        lift[0:64, i * 256 : (i + 1) * 256] = block
        lift[64:128, i * 256 : (i + 1) * 256] = block
    l_level.wait()
    weights[0:128, 0:128] = jnp.zeros((128, 128), BF16)
    for t in range(1, LEVELS):
        weights[0:128, t * 128 : (t + 1) * 128] = twice(level_own[t])
    l_coup.wait()
    for t in range(LEVELS):
        pair_coup[t] = twice(coup[t])
    drain(level_sib, recv.at[1])
    for t in range(LEVELS):
        weights[128:256, t * 128 : (t + 1) * 128] = twice(level_sib[t])
    drain(xs.at[pl.ds(0, 4)], loc.at[15])

    def block_of(g):
        parts = [xs[s * 4 + g].astype(F32) for s in range(4)]
        return jnp.concatenate(parts, axis=0).astype(BF16)

    low = lax.broadcasted_iota(jnp.int32, (8, 128), 1) < 64

    drain(xs.at[pl.ds(0, 3)], recv.at[0])
    own = block_of(q)
    part = dot(own, lift[...], NT)
    roots[q] = jnp.where(low, part[0:8], part[8:16])
    for dev in by_root[:3]:
        push(roots.at[q], roots.at[q], 3, dev)
    for dev in by_root[3:]:
        push(roots.at[q], roots.at[4 + q], 3, dev)
    pl.semaphore_wait(token.at[0], len(close))
    for dev in row:
        pl.semaphore_signal(token.at[1], inc=1, device_id=dev, device_id_type=MESH)
    for d in (1, 2, 3):
        for p in x_peers:
            g = lax.rem(p + d, NX)
            push(chunk(g), xs.at[q * 4 + g], 2, (leaf, p))

    own_x[...] = own
    mine = 16 + q * 4
    for i in range(4):
        two = [
            dot(own_x[:, l * 256 : (l + 1) * 256], basis[l], NT) for l in (2 * i, 2 * i + 1)
        ]
        coefs[mine + i] = jnp.concatenate(two, axis=1).astype(BF16)

    drain(roots.at[pl.ds(0, 7)], recv.at[3])
    root_own = (roots[0] + roots[1]) + (roots[2] + roots[3])
    root_sib = (roots[4] + roots[5]) + (roots[6] + roots[7])
    both = jnp.concatenate([root_own, root_sib], axis=1).astype(BF16)
    sums = dot(both, weights[...])
    for t in range(1, LEVELS):
        term = sums[:, t * 128 : (t + 1) * 128] * (2.0 ** (-0.5 * t))
        terms[t - 1] = term.astype(BF16)
    pl.semaphore_wait(token.at[1], len(row))
    for d in FARTHEST_FIRST:
        t = d.bit_length()
        dev = (leaf_at(flipped(z, d // NY), flipped(y, d % NY), core), q)
        push(terms.at[t - 1], tree.at[d], 5, dev, tree_recv.at[t - 1])
    src = coefs.at[pl.ds(mine, 4)]
    for dev in by_root[:3]:
        push(src, src, 4, dev)
    for d in range(4):
        p = lax.rem(q + d, NX)
        push(src, coefs.at[pl.ds(q * 4, 4)], 4, (up, p))
        push(src, coefs.at[pl.ds(32 + q * 4, 4)], 4, (down, p))

    coupled = dot(sums[:, 0:128].astype(BF16), pair_coup[0], NT)
    drain(xs.at[pl.ds(0, 9)], recv.at[2])
    for g in range(4):
        group = block_of(g)
        for i in range(8):
            x16[g * 8 + i] = group[:, i * 256 : (i + 1) * 256]
    l_nl.wait()
    l_near.wait()
    for i in range(8):
        total = None
        for n in range(2):
            at = jnp.clip(near_l[n, i] - leaf * 32, 0, 31)
            one = dot(x16[at], near_b[i, n], NT)
            total = one if total is None else total + one
        local_out[:, i * 256 : (i + 1) * 256] = total
    l_fl.wait()
    l_fc.wait()
    l_far.wait()
    drain(coefs.at[pl.ds(0, 44)], recv.at[4])
    for i in range(8):
        total = None
        for f in range(6):
            at = jnp.clip(far_l[f, q * 8 + i] - leaf * 32 + 32, 0, 95)
            pair = coefs[at // 2].astype(F32)
            odd = jnp.full((16, 64), lax.rem(at, 2), jnp.int32) == 1
            used = jnp.full((16, 64), far_c[q * 8 + i], jnp.int32) > f
            value = jnp.where(odd, pair[:, 64:], pair[:, :64])
            value = jnp.where(used, value, 0.0).astype(BF16)
            one = dot(value, far_b[i, f], NT)
            total = one if total is None else total + one
        local_out[:, i * 256 : (i + 1) * 256] += dot(total.astype(BF16), basis[i])

    for t in range(1, LEVELS):
        lo, hi = 1 << (t - 1), 1 << t
        drain(tree.at[pl.ds(lo, hi - lo)], tree_recv.at[t - 1])
        blocks = [tree[d].astype(F32) for d in range(lo, hi)]
        while len(blocks) > 1:
            blocks = [a + b for a, b in zip(blocks[0::2], blocks[1::2])]
        coupled = coupled + dot(blocks[0].astype(BF16), pair_coup[t], NT)
    spread = jnp.concatenate(
        [jnp.where(low, coupled, 0.0), jnp.where(low, 0.0, coupled)], axis=0
    ).astype(BF16)
    for h in range(2):
        cols = slice(h * 1024, (h + 1) * 1024)
        total = dot(spread, lift[:, cols]) + local_out[:, cols]
        for p in range(4):
            result[p, :, cols] = total[4 * p : 4 * p + 4].astype(BF16)
        for p in x_peers:
            push(result.at[p, :, cols], out.at[q, :, cols], 6, (leaf, p))
    last = pltpu.make_async_copy(result.at[q], out.at[q], loc.at[14])
    last.start()
    drain(xs.at[pl.ds(0, 3)], send.at[0])
    drain(level_sib, send.at[1])
    drain(xs.at[pl.ds(0, 9)], send.at[2])
    drain(roots.at[pl.ds(0, 7)], send.at[3])
    drain(coefs.at[pl.ds(0, 44)], send.at[4])
    drain(tree.at[pl.ds(1, NY * NZ - 1)], send.at[5])
    drain(result.at[pl.ds(0, 3)], send.at[6])
    last.wait()
    drain(result.at[pl.ds(0, 3)], recv.at[6])


def local(
    vectors,
    near_blocks,
    near_list,
    bases,
    leaf_maps,
    far_blocks,
    far_list,
    far_count,
    level_maps,
    coupling,
):
    gathered = pl.pallas_call(
        kernel,
        out_shape=jax.ShapeDtypeStruct((4, 4, 2048), BF16),
        in_specs=[pl.BlockSpec(memory_space=pl.ANY)] * 10,
        out_specs=pl.BlockSpec(memory_space=pl.ANY),
        scratch_shapes=[
            pltpu.VMEM((16, 4, 2048), BF16),
            pltpu.VMEM((16, 2048), BF16),
            pltpu.VMEM((32, 16, 256), BF16),
            pltpu.VMEM((8, 2, 256, 256), BF16),
            pltpu.SMEM((2, 8), jnp.int32),
            pltpu.VMEM((8, 64, 256), BF16),
            pltpu.VMEM((8, 64, 64), BF16),
            pltpu.VMEM((8, 6, 64, 64), BF16),
            pltpu.SMEM((6, 32), jnp.int32),
            pltpu.SMEM((32,), jnp.int32),
            pltpu.VMEM((LEVELS, 64, 64), BF16),
            pltpu.VMEM((LEVELS, 64, 64), BF16),
            pltpu.VMEM((LEVELS, 64, 64), BF16),
            pltpu.VMEM((128, 2048), BF16),
            pltpu.VMEM((256, LEVELS * 128), BF16),
            pltpu.VMEM((LEVELS, 128, 128), BF16),
            pltpu.VMEM((8, 8, 128), F32),
            pltpu.VMEM((48, 16, 128), BF16),
            pltpu.VMEM((LEVELS - 1, 8, 128), BF16),
            pltpu.VMEM((NY * NZ, 8, 128), BF16),
            pltpu.VMEM((16, 2048), F32),
            pltpu.VMEM((4, 4, 2048), BF16),
            pltpu.SemaphoreType.DMA((16,)),
            pltpu.SemaphoreType.DMA((7,)),
            pltpu.SemaphoreType.DMA((7,)),
            pltpu.SemaphoreType.DMA((LEVELS - 1,)),
            pltpu.SemaphoreType.REGULAR((2,)),
        ],
        compiler_params=pltpu.CompilerParams(
            collective_id=0, has_side_effects=True, vmem_limit_bytes=64 * 2**20
        ),
        name="h2_product",
    )(
        vectors,
        near_blocks,
        near_list.T,
        bases.transpose(0, 2, 1),
        leaf_maps,
        far_blocks,
        far_list.T,
        far_count,
        level_maps,
        coupling,
    )
    return gathered.astype(F32).transpose(1, 0, 2).reshape(4, 8192)


def solution(mesh):
    in_specs = (
        P("vec", "leaf"),
        P(("leaf", "vec"), None, None, None),
        P(("leaf", "vec"), None),
        P(("leaf", "vec"), None, None),
        P("leaf", None, None),
        P("leaf", None, None, None),
        P("leaf", None),
        P("leaf"),
        P("leaf", None, None, None),
        P("leaf", None, None, None),
    )
    return jax.shard_map(
        local, mesh=mesh, in_specs=in_specs, out_specs=P("vec", "leaf"), check_vma=False
    )
```

```python
import functools

import jax
import jax.numpy as jnp
from jax import lax
from jax.experimental import pallas as pl
from jax.experimental.pallas import tpu as pltpu
from jax.sharding import PartitionSpec as P

MESH = pl.DeviceIdType.MESH
F32 = jnp.float32
BF16 = jnp.bfloat16
NN = (((1,), (0,)), ((), ()))
NT = (((1,), (1,)), ((), ()))
TN = (((0,), (0,)), ((), ()))
NX, NY, NZ = 4, 8, 8
LEVELS = 7


def dot(a, b, dims=NN):
    return lax.dot_general(a, b, dims, preferred_element_type=F32)


def drain(ref, sem):
    pltpu.make_async_copy(ref, ref, sem).wait()


def flipped(value, mask):
    out = 0
    for b in range(3):
        bit = lax.rem(value // (1 << b), 2)
        out = out + (1 << b) * ((1 - bit) if (mask >> b) & 1 else bit)
    return out


def twice(block):
    zero = jnp.zeros_like(block)
    return jnp.concatenate(
        [jnp.concatenate([block, zero], axis=1), jnp.concatenate([zero, block], axis=1)],
        axis=0,
    )


REACH = (0, 1, 2, 3, 4, 3, 2, 3)
FARTHEST_FIRST = sorted(range(1, NY * NZ), key=lambda d: -(REACH[d // NY] + REACH[d % NY]))


def kernel(
    vectors,
    near_blocks,
    near_list,
    bases,
    leaf_maps,
    far_blocks,
    far_list,
    far_count,
    level_maps,
    coupling,
    out,
    xs,
    own_x,
    x16,
    near_b,
    near_l,
    basis,
    maps,
    far_b,
    far_l,
    far_c,
    level_own,
    level_sib,
    coup,
    lift,
    weights,
    pair_coup,
    roots,
    coefs,
    terms,
    tree,
    local_out,
    result,
    loc,
    send,
    recv,
    tree_recv,
    token,
):
    leaf = lax.axis_index("leaf")
    q = lax.axis_index("vec")
    core = lax.rem(leaf, 2)
    chip = leaf // 2
    y = lax.rem(chip, NY)
    z = chip // NY

    def leaf_at(zz, yy, cc):
        return (zz * NY + yy) * 2 + cc

    sib = leaf_at(z, y, 1 - core)
    off_chip = lax.rem(leaf + 2 * NY * NZ - 1 + 2 * core, 2 * NY * NZ)
    off_slot = 32 - 32 * core
    x_peers = [lax.rem(q + d, NX) for d in (1, 2, 3)]
    by_root = [(leaf, p) for p in x_peers] + [(sib, lax.rem(q + d, NX)) for d in range(4)]
    steps = (1, 2, NY - 2, NY - 1)
    close = [(leaf_at(z, lax.rem(y + d, NY), core), q) for d in steps]
    close += [(leaf_at(lax.rem(z + d, NZ), y, core), q) for d in steps]
    close += [(off_chip, q)]
    row = [(leaf_at(z, lax.rem(y + d, NY), core), q) for d in range(1, NY)]

    barrier = pltpu.get_barrier_semaphore()
    for dev in by_root + close:
        pl.semaphore_signal(barrier, inc=1, device_id=dev, device_id_type=MESH)

    copies = []

    def load(src, dst):
        c = pltpu.make_async_copy(src, dst, loc.at[len(copies)])
        c.start()
        copies.append(c)
        return c

    l_basis = load(bases, basis)
    l_maps = load(leaf_maps.at[pl.ds(q * 8, 8)], maps)
    for g in range(4):
        pltpu.make_async_copy(
            vectors.at[:, pl.ds(g * 2048, 2048)], xs.at[q * 4 + g], loc.at[15]
        ).start()
    l_level = load(level_maps.at[0], level_own)
    l_coup = load(coupling.at[0], coup)
    l_nl = load(near_list, near_l)
    l_fl = load(far_list, far_l)
    l_fc = load(far_count, far_c)
    l_near = load(near_blocks, near_b)
    l_far = load(far_blocks.at[pl.ds(q * 8, 8)], far_b)

    pl.semaphore_wait(barrier, len(by_root + close))

    def push(src, dst, k, dev, rsem=None):
        pltpu.make_async_remote_copy(
            src_ref=src,
            dst_ref=dst,
            send_sem=send.at[k],
            recv_sem=recv.at[k] if rsem is None else rsem,
            device_id=dev,
            device_id_type=MESH,
        ).start()

    def chunk(g):
        return xs.at[q * 4 + g]

    drain(xs.at[pl.ds(0, 4)], loc.at[15])
    for p in x_peers:
        push(chunk(p), xs.at[q * 4 + p], 0, (leaf, p))
    push(level_maps.at[0], level_sib, 1, (sib, q))
    for dev in close:
        pl.semaphore_signal(token.at[0], inc=1, device_id=dev, device_id_type=MESH)

    l_basis.wait()
    l_maps.wait()
    for i in range(8):
        block = dot(maps[i], basis[i], TN).astype(BF16)
        lift[0:64, i * 256 : (i + 1) * 256] = block
        lift[64:128, i * 256 : (i + 1) * 256] = block
    l_level.wait()
    weights[0:128, 0:128] = jnp.zeros((128, 128), BF16)
    for t in range(1, LEVELS):
        weights[0:128, t * 128 : (t + 1) * 128] = twice(level_own[t])
    l_coup.wait()
    for t in range(LEVELS):
        pair_coup[t] = twice(coup[t])
    drain(level_sib, recv.at[1])
    for t in range(LEVELS):
        weights[128:256, t * 128 : (t + 1) * 128] = twice(level_sib[t])

    def block_of(g):
        parts = [xs[s * 4 + g].astype(F32) for s in range(4)]
        return jnp.concatenate(parts, axis=0).astype(BF16)

    low = lax.broadcasted_iota(jnp.int32, (8, 128), 1) < 64

    drain(xs.at[pl.ds(0, 3)], recv.at[0])
    own = block_of(q)
    part = dot(own, lift[...], NT)
    roots[q] = jnp.where(low, part[0:8], part[8:16])
    for dev in by_root[:3]:
        push(roots.at[q], roots.at[q], 3, dev)
    for dev in by_root[3:]:
        push(roots.at[q], roots.at[4 + q], 3, dev)
    pl.semaphore_wait(token.at[0], len(close))
    for dev in row:
        pl.semaphore_signal(token.at[1], inc=1, device_id=dev, device_id_type=MESH)
    for d in (1, 2, 3):
        for p in x_peers:
            g = lax.rem(p + d, NX)
            push(chunk(g), xs.at[q * 4 + g], 2, (leaf, p))

    own_x[...] = own
    mine = 16 + q * 4
    for i in range(4):
        two = [
            dot(own_x[:, l * 256 : (l + 1) * 256], basis[l], NT) for l in (2 * i, 2 * i + 1)
        ]
        coefs[mine + i] = jnp.concatenate(two, axis=1).astype(BF16)

    src = coefs.at[pl.ds(mine, 4)]
    for dev in by_root[:3]:
        push(src, src, 4, dev)
    for dev in by_root[3:]:
        push(src, coefs.at[pl.ds(32 - off_slot + q * 4, 4)], 4, dev)
    for d in range(4):
        push(src, coefs.at[pl.ds(off_slot + q * 4, 4)], 4, (off_chip, lax.rem(q + d, NX)))

    drain(roots.at[pl.ds(0, 7)], recv.at[3])
    root_own = (roots[0] + roots[1]) + (roots[2] + roots[3])
    root_sib = (roots[4] + roots[5]) + (roots[6] + roots[7])
    both = jnp.concatenate([root_own, root_sib], axis=1).astype(BF16)
    sums = dot(both, weights[...])
    for t in range(1, LEVELS):
        term = sums[:, t * 128 : (t + 1) * 128] * (2.0 ** (-0.5 * t))
        terms[t - 1] = term.astype(BF16)
    pl.semaphore_wait(token.at[1], len(row))
    for d in FARTHEST_FIRST:
        t = d.bit_length()
        dev = (leaf_at(flipped(z, d // NY), flipped(y, d % NY), core), q)
        push(terms.at[t - 1], tree.at[d], 5, dev, tree_recv.at[t - 1])

    coupled = dot(sums[:, 0:128].astype(BF16), pair_coup[0], NT)
    drain(xs.at[pl.ds(0, 9)], recv.at[2])
    for g in range(4):
        group = block_of(g)
        for i in range(8):
            x16[g * 8 + i] = group[:, i * 256 : (i + 1) * 256]
    l_nl.wait()
    l_near.wait()
    for i in range(8):
        total = None
        for n in range(2):
            at = jnp.clip(near_l[n, i] - leaf * 32, 0, 31)
            one = dot(x16[at], near_b[i, n], NT)
            total = one if total is None else total + one
        local_out[:, i * 256 : (i + 1) * 256] = total
    l_fl.wait()
    l_fc.wait()
    l_far.wait()
    drain(coefs.at[pl.ds(0, 44)], recv.at[4])
    for i in range(8):
        total = None
        for f in range(6):
            at = jnp.clip(far_l[f, q * 8 + i] - leaf * 32 + 32, 0, 95)
            pair = coefs[at // 2].astype(F32)
            odd = jnp.full((16, 64), lax.rem(at, 2), jnp.int32) == 1
            used = jnp.full((16, 64), far_c[q * 8 + i], jnp.int32) > f
            value = jnp.where(odd, pair[:, 64:], pair[:, :64])
            value = jnp.where(used, value, 0.0).astype(BF16)
            one = dot(value, far_b[i, f], NT)
            total = one if total is None else total + one
        local_out[:, i * 256 : (i + 1) * 256] += dot(total.astype(BF16), basis[i])

    for t in range(1, LEVELS):
        lo, hi = 1 << (t - 1), 1 << t
        drain(tree.at[pl.ds(lo, hi - lo)], tree_recv.at[t - 1])
        blocks = [tree[d].astype(F32) for d in range(lo, hi)]
        while len(blocks) > 1:
            blocks = [a + b for a, b in zip(blocks[0::2], blocks[1::2])]
        coupled = coupled + dot(blocks[0].astype(BF16), pair_coup[t], NT)
    spread = jnp.concatenate(
        [jnp.where(low, coupled, 0.0), jnp.where(low, 0.0, coupled)], axis=0
    ).astype(BF16)
    for h in range(2):
        cols = slice(h * 1024, (h + 1) * 1024)
        total = dot(spread, lift[:, cols]) + local_out[:, cols]
        for p in range(4):
            result[p, :, cols] = total[4 * p : 4 * p + 4].astype(BF16)
        for p in x_peers:
            push(result.at[p, :, cols], out.at[q, :, cols], 6, (leaf, p))
    last = pltpu.make_async_copy(result.at[q], out.at[q], loc.at[14])
    last.start()
    drain(xs.at[pl.ds(0, 3)], send.at[0])
    drain(level_sib, send.at[1])
    drain(xs.at[pl.ds(0, 9)], send.at[2])
    drain(roots.at[pl.ds(0, 7)], send.at[3])
    drain(coefs.at[pl.ds(0, 44)], send.at[4])
    drain(tree.at[pl.ds(1, NY * NZ - 1)], send.at[5])
    drain(result.at[pl.ds(0, 3)], send.at[6])
    last.wait()
    drain(result.at[pl.ds(0, 3)], recv.at[6])


def local(
    vectors,
    near_blocks,
    near_list,
    bases,
    leaf_maps,
    far_blocks,
    far_list,
    far_count,
    level_maps,
    coupling,
):
    operands = (
        vectors,
        near_blocks,
        near_list.T,
        bases.transpose(0, 2, 1),
        leaf_maps,
        far_blocks,
        far_list.T,
        far_count,
        level_maps,
        coupling,
    )
    gathered = pl.pallas_call(
        kernel,
        out_shape=pltpu.VMEM((4, 4, 2048), BF16),
        in_specs=[pl.BlockSpec(memory_space=pl.ANY)] * 10,
        out_specs=pl.BlockSpec(memory_space=pltpu.VMEM),
        scratch_shapes=[
            pltpu.VMEM((16, 4, 2048), BF16),
            pltpu.VMEM((16, 2048), BF16),
            pltpu.VMEM((32, 16, 256), BF16),
            pltpu.VMEM((8, 2, 256, 256), BF16),
            pltpu.SMEM((2, 8), jnp.int32),
            pltpu.VMEM((8, 64, 256), BF16),
            pltpu.VMEM((8, 64, 64), BF16),
            pltpu.VMEM((8, 6, 64, 64), BF16),
            pltpu.SMEM((6, 32), jnp.int32),
            pltpu.SMEM((32,), jnp.int32),
            pltpu.VMEM((LEVELS, 64, 64), BF16),
            pltpu.VMEM((LEVELS, 64, 64), BF16),
            pltpu.VMEM((LEVELS, 64, 64), BF16),
            pltpu.VMEM((128, 2048), BF16),
            pltpu.VMEM((256, LEVELS * 128), BF16),
            pltpu.VMEM((LEVELS, 128, 128), BF16),
            pltpu.VMEM((8, 8, 128), F32),
            pltpu.VMEM((48, 16, 128), BF16),
            pltpu.VMEM((LEVELS - 1, 8, 128), BF16),
            pltpu.VMEM((NY * NZ, 8, 128), BF16),
            pltpu.VMEM((16, 2048), F32),
            pltpu.VMEM((4, 4, 2048), BF16),
            pltpu.SemaphoreType.DMA((16,)),
            pltpu.SemaphoreType.DMA((7,)),
            pltpu.SemaphoreType.DMA((7,)),
            pltpu.SemaphoreType.DMA((LEVELS - 1,)),
            pltpu.SemaphoreType.REGULAR((2,)),
        ],
        compiler_params=pltpu.CompilerParams(
            collective_id=0, has_side_effects=True, vmem_limit_bytes=48 * 2**20
        ),
        name="h2_product",
    )(*(pltpu.with_memory_space_constraint(a, pltpu.HBM) for a in operands))
    return gathered.astype(F32).transpose(1, 0, 2).reshape(4, 8192)


def solution(mesh):
    in_specs = (
        P("vec", "leaf"),
        P(("leaf", "vec"), None, None, None),
        P(("leaf", "vec"), None),
        P(("leaf", "vec"), None, None),
        P("leaf", None, None),
        P("leaf", None, None, None),
        P("leaf", None),
        P("leaf"),
        P("leaf", None, None, None),
        P("leaf", None, None, None),
    )
    return jax.shard_map(
        local, mesh=mesh, in_specs=in_specs, out_specs=P("vec", "leaf"), check_vma=False
    )
```

```python
import functools

import jax
import jax.numpy as jnp
from jax import lax
from jax.experimental import pallas as pl
from jax.experimental.pallas import tpu as pltpu
from jax.sharding import PartitionSpec as P

MESH = pl.DeviceIdType.MESH
F32 = jnp.float32
BF16 = jnp.bfloat16
NN = (((1,), (0,)), ((), ()))
NT = (((1,), (1,)), ((), ()))
TN = (((0,), (0,)), ((), ()))
NX, NY, NZ = 4, 8, 8
LEVELS = 7


def dot(a, b, dims=NN):
    return lax.dot_general(a, b, dims, preferred_element_type=F32)


def drain(ref, sem):
    pltpu.make_async_copy(ref, ref, sem).wait()


def flipped(value, mask):
    out = 0
    for b in range(3):
        bit = lax.rem(value // (1 << b), 2)
        out = out + (1 << b) * ((1 - bit) if (mask >> b) & 1 else bit)
    return out


def twice(block):
    zero = jnp.zeros_like(block)
    return jnp.concatenate(
        [jnp.concatenate([block, zero], axis=1), jnp.concatenate([zero, block], axis=1)],
        axis=0,
    )


REACH = (0, 1, 2, 3, 4, 3, 2, 3)
FARTHEST_FIRST = sorted(range(1, NY * NZ), key=lambda d: -(REACH[d // NY] + REACH[d % NY]))


def kernel(
    vectors,
    near_blocks,
    near_list,
    bases,
    leaf_maps,
    far_blocks,
    far_list,
    far_count,
    level_maps,
    coupling,
    out,
    xs,
    own_x,
    x16,
    near_b,
    near_l,
    basis,
    maps,
    far_b,
    far_l,
    far_c,
    level_own,
    level_sib,
    coup,
    lift,
    lifts,
    weights,
    pair_coup,
    roots,
    coefs,
    terms,
    tree,
    local_out,
    result,
    parts,
    loc,
    send,
    recv,
    tree_recv,
    token,
):
    leaf = lax.axis_index("leaf")
    q = lax.axis_index("vec")
    core = lax.rem(leaf, 2)
    chip = leaf // 2
    y = lax.rem(chip, NY)
    z = chip // NY

    def leaf_at(zz, yy, cc):
        return (zz * NY + yy) * 2 + cc

    sib = leaf_at(z, y, 1 - core)
    off_chip = leaf - 1 + 2 * core
    off_slot = 32 - 32 * core
    has_off = jnp.logical_and(leaf > 0, leaf < 2 * NY * NZ - 1)
    x_peers = [lax.rem(q + d, NX) for d in (1, 2, 3)]
    by_root = [(leaf, p) for p in x_peers] + [(sib, lax.rem(q + d, NX)) for d in range(4)]
    steps = (1, 2, NY - 2, NY - 1)
    close = [(leaf_at(z, lax.rem(y + d, NY), core), q) for d in steps]
    inside = [
        (z >= 2, (leaf_at(z - 2, y, core), q)),
        (z >= 1, (leaf_at(z - 1, y, core), q)),
        (z < NZ - 1, (leaf_at(z + 1, y, core), q)),
        (z < NZ - 2, (leaf_at(z + 2, y, core), q)),
        (has_off, (off_chip, q)),
    ]
    n_close = len(close) + sum(jnp.where(ok, 1, 0) for ok, _ in inside)
    opposite = (leaf_at(lax.rem(z + NZ // 2, NZ), y, core), q)
    early = z < NZ // 2
    row = [(leaf_at(z, lax.rem(y + d, NY), core), q) for d in range(1, NY)]

    barrier = pltpu.get_barrier_semaphore()

    def greet(sem, devs):
        for dev in devs:
            pl.semaphore_signal(sem, inc=1, device_id=dev, device_id_type=MESH)

    def greet_close(sem):
        greet(sem, close)
        for ok, dev in inside:
            pl.when(ok)(functools.partial(greet, sem, [dev]))

    greet(barrier, by_root)
    greet_close(barrier)

    copies = []

    def load(src, dst):
        c = pltpu.make_async_copy(src, dst, loc.at[len(copies)])
        c.start()
        copies.append(c)
        return c

    l_basis = load(bases, basis)
    l_maps = load(leaf_maps.at[pl.ds(q * 8, 8)], maps)
    for g in range(4):
        pltpu.make_async_copy(
            vectors.at[:, pl.ds(g * 2048, 2048)], xs.at[q * 4 + g], loc.at[15]
        ).start()
    l_level = load(level_maps.at[0], level_own)
    l_coup = load(coupling.at[0], coup)
    l_nl = load(near_list, near_l)
    l_fl = load(far_list, far_l)
    l_fc = load(far_count, far_c)
    l_near = load(near_blocks, near_b)
    l_far = load(far_blocks.at[pl.ds(q * 8, 8)], far_b)

    pl.semaphore_wait(barrier, len(by_root) + n_close)

    def push(src, dst, k, dev, rsem=None):
        pltpu.make_async_remote_copy(
            src_ref=src,
            dst_ref=dst,
            send_sem=send.at[k],
            recv_sem=recv.at[k] if rsem is None else rsem,
            device_id=dev,
            device_id_type=MESH,
        ).start()

    def chunk(g):
        return xs.at[q * 4 + g]

    drain(xs.at[pl.ds(0, 4)], loc.at[15])
    for p in x_peers:
        push(chunk(p), xs.at[q * 4 + p], 0, (leaf, p))
    push(level_maps.at[0], level_sib, 1, (sib, q))
    greet_close(token.at[0])

    l_basis.wait()
    l_maps.wait()
    for i in range(8):
        block = dot(maps[i], basis[i], TN).astype(BF16)
        lift[0:64, i * 256 : (i + 1) * 256] = block
        lift[64:128, i * 256 : (i + 1) * 256] = block
        lifts[q, :, i * 256 : (i + 1) * 256] = block
    l_level.wait()
    weights[0:128, 0:128] = jnp.zeros((128, 128), BF16)
    for t in range(1, LEVELS):
        weights[0:128, t * 128 : (t + 1) * 128] = twice(level_own[t])
    l_coup.wait()
    for t in range(LEVELS):
        pair_coup[t] = twice(coup[t])
    drain(level_sib, recv.at[1])
    for t in range(LEVELS):
        weights[128:256, t * 128 : (t + 1) * 128] = twice(level_sib[t])

    def block_of(g):
        parts = [xs[s * 4 + g].astype(F32) for s in range(4)]
        return jnp.concatenate(parts, axis=0).astype(BF16)

    pl.semaphore_wait(token.at[0], n_close)
    greet(token.at[1], [opposite])

    low = lax.broadcasted_iota(jnp.int32, (8, 128), 1) < 64

    drain(xs.at[pl.ds(0, 3)], recv.at[0])
    own = block_of(q)
    part = dot(own, lift[...], NT)
    roots[q] = jnp.where(low, part[0:8], part[8:16])
    for dev in by_root[:3]:
        push(roots.at[q], roots.at[q], 3, dev)
    for dev in by_root[3:]:
        push(roots.at[q], roots.at[4 + q], 3, dev)
    for d in (1, 2, 3):
        for p in x_peers:
            g = lax.rem(p + d, NX)
            push(chunk(g), xs.at[q * 4 + g], 2, (leaf, p))

    own_x[...] = own
    mine = 16 + q * 4
    for i in range(4):
        two = [
            dot(own_x[:, l * 256 : (l + 1) * 256], basis[l], NT) for l in (2 * i, 2 * i + 1)
        ]
        coefs[mine + i] = jnp.concatenate(two, axis=1).astype(BF16)

    src = coefs.at[pl.ds(mine, 4)]
    for dev in by_root[:3]:
        push(src, src, 4, dev)
    for dev in by_root[3:]:
        push(src, coefs.at[pl.ds(32 - off_slot + q * 4, 4)], 4, dev)

    @pl.when(has_off)
    def _():
        for d in range(4):
            push(src, coefs.at[pl.ds(off_slot + q * 4, 4)], 8, (off_chip, lax.rem(q + d, NX)))

    @pl.when(jnp.logical_not(has_off))
    def _():
        coefs[pl.ds(32 * core, 16)] = jnp.zeros((16, 16, 128), BF16)

    def share_lift():
        for p in x_peers:
            push(lifts.at[q], lifts.at[q], 6, (leaf, p))

    pl.when(early)(share_lift)
    pl.semaphore_wait(token.at[1], 1)
    greet(token.at[2], row)

    drain(roots.at[pl.ds(0, 7)], recv.at[3])
    root_own = (roots[0] + roots[1]) + (roots[2] + roots[3])
    root_sib = (roots[4] + roots[5]) + (roots[6] + roots[7])
    both = jnp.concatenate([root_own, root_sib], axis=1).astype(BF16)
    sums = dot(both, weights[...])
    for t in range(1, LEVELS):
        term = sums[:, t * 128 : (t + 1) * 128] * (2.0 ** (-0.5 * t))
        terms[t - 1] = term.astype(BF16)
    pl.semaphore_wait(token.at[2], len(row))
    for d in FARTHEST_FIRST:
        t = d.bit_length()
        dev = (leaf_at(flipped(z, d // NY), flipped(y, d % NY), core), q)
        push(terms.at[t - 1], tree.at[d], 5, dev, tree_recv.at[t - 1])
    pl.when(jnp.logical_not(early))(share_lift)

    coupled = dot(sums[:, 0:128].astype(BF16), pair_coup[0], NT)
    drain(xs.at[pl.ds(0, 9)], recv.at[2])
    for g in range(4):
        group = block_of(g)
        for i in range(8):
            x16[g * 8 + i] = group[:, i * 256 : (i + 1) * 256]
    l_nl.wait()
    l_near.wait()
    for i in range(8):
        total = None
        for n in range(2):
            at = jnp.clip(near_l[n, i] - leaf * 32, 0, 31)
            one = dot(x16[at], near_b[i, n], NT)
            total = one if total is None else total + one
        local_out[:, i * 256 : (i + 1) * 256] = total
    l_fl.wait()
    l_fc.wait()
    l_far.wait()
    drain(coefs.at[pl.ds(0, 28)], recv.at[4])

    @pl.when(has_off)
    def _():
        drain(coefs.at[pl.ds(0, 16)], recv.at[8])

    for i in range(8):
        total = None
        for f in range(6):
            at = jnp.clip(far_l[f, q * 8 + i] - leaf * 32 + 32, 0, 95)
            pair = coefs[at // 2].astype(F32)
            odd = jnp.full((16, 64), lax.rem(at, 2), jnp.int32) == 1
            used = jnp.full((16, 64), far_c[q * 8 + i], jnp.int32) > f
            value = jnp.where(odd, pair[:, 64:], pair[:, :64])
            value = jnp.where(used, value, 0.0).astype(BF16)
            one = dot(value, far_b[i, f], NT)
            total = one if total is None else total + one
        cols = slice(i * 256, (i + 1) * 256)
        total = local_out[:, cols] + dot(total.astype(BF16), basis[i])
        for p in range(4):
            result[p, :, cols] = total[4 * p : 4 * p + 4].astype(BF16)
    for p in x_peers:
        push(result.at[p], parts.at[q], 7, (leaf, p))
    parts[q] = result[q]

    for t in range(1, LEVELS):
        lo, hi = 1 << (t - 1), 1 << t
        drain(tree.at[pl.ds(lo, hi - lo)], tree_recv.at[t - 1])
        blocks = [tree[d].astype(F32) for d in range(lo, hi)]
        while len(blocks) > 1:
            blocks = [a + b for a, b in zip(blocks[0::2], blocks[1::2])]
        coupled = coupled + dot(blocks[0].astype(BF16), pair_coup[t], NT)
    half = jnp.where(jnp.full((8, 64), q, jnp.int32) < 2, coupled[:, :64], coupled[:, 64:])
    turned = jnp.concatenate([half[4:8], half[0:4]], axis=0)
    odd = jnp.full((8, 64), lax.rem(q, 2), jnp.int32) == 1
    mine4 = jnp.where(odd, turned, half).astype(BF16)
    drain(lifts.at[pl.ds(0, 3)], recv.at[6])
    drain(parts.at[pl.ds(0, 3)], recv.at[7])
    for g in range(4):
        up_part = dot(mine4, lifts[g])
        out[:, g * 2048 : (g + 1) * 2048] = up_part[0:4] + parts[g].astype(F32)
    drain(xs.at[pl.ds(0, 3)], send.at[0])
    drain(level_sib, send.at[1])
    drain(xs.at[pl.ds(0, 9)], send.at[2])
    drain(roots.at[pl.ds(0, 7)], send.at[3])
    drain(coefs.at[pl.ds(0, 28)], send.at[4])

    @pl.when(has_off)
    def _():
        drain(coefs.at[pl.ds(0, 16)], send.at[8])

    drain(tree.at[pl.ds(1, NY * NZ - 1)], send.at[5])
    drain(lifts.at[pl.ds(0, 3)], send.at[6])
    drain(parts.at[pl.ds(0, 3)], send.at[7])


def local(
    vectors,
    near_blocks,
    near_list,
    bases,
    leaf_maps,
    far_blocks,
    far_list,
    far_count,
    level_maps,
    coupling,
):
    operands = (
        vectors,
        near_blocks,
        near_list.T,
        bases.transpose(0, 2, 1),
        leaf_maps,
        far_blocks,
        far_list.T,
        far_count,
        level_maps,
        coupling,
    )
    return pl.pallas_call(
        kernel,
        out_shape=pltpu.VMEM((4, 8192), F32),
        in_specs=[pl.BlockSpec(memory_space=pl.ANY)] * 10,
        out_specs=pl.BlockSpec(memory_space=pltpu.VMEM),
        scratch_shapes=[
            pltpu.VMEM((16, 4, 2048), BF16),
            pltpu.VMEM((16, 2048), BF16),
            pltpu.VMEM((32, 16, 256), BF16),
            pltpu.VMEM((8, 2, 256, 256), BF16),
            pltpu.SMEM((2, 8), jnp.int32),
            pltpu.VMEM((8, 64, 256), BF16),
            pltpu.VMEM((8, 64, 64), BF16),
            pltpu.VMEM((8, 6, 64, 64), BF16),
            pltpu.SMEM((6, 32), jnp.int32),
            pltpu.SMEM((32,), jnp.int32),
            pltpu.VMEM((LEVELS, 64, 64), BF16),
            pltpu.VMEM((LEVELS, 64, 64), BF16),
            pltpu.VMEM((LEVELS, 64, 64), BF16),
            pltpu.VMEM((128, 2048), BF16),
            pltpu.VMEM((4, 64, 2048), BF16),
            pltpu.VMEM((256, LEVELS * 128), BF16),
            pltpu.VMEM((LEVELS, 128, 128), BF16),
            pltpu.VMEM((8, 8, 128), F32),
            pltpu.VMEM((48, 16, 128), BF16),
            pltpu.VMEM((LEVELS - 1, 8, 128), BF16),
            pltpu.VMEM((NY * NZ, 8, 128), BF16),
            pltpu.VMEM((16, 2048), F32),
            pltpu.VMEM((4, 4, 2048), BF16),
            pltpu.VMEM((4, 4, 2048), BF16),
            pltpu.SemaphoreType.DMA((16,)),
            pltpu.SemaphoreType.DMA((9,)),
            pltpu.SemaphoreType.DMA((9,)),
            pltpu.SemaphoreType.DMA((LEVELS - 1,)),
            pltpu.SemaphoreType.REGULAR((3,)),
        ],
        compiler_params=pltpu.CompilerParams(
            collective_id=0, has_side_effects=True, vmem_limit_bytes=48 * 2**20
        ),
        name="h2_product",
    )(*(pltpu.with_memory_space_constraint(a, pltpu.HBM) for a in operands))


def solution(mesh):
    in_specs = (
        P("vec", "leaf"),
        P(("leaf", "vec"), None, None, None),
        P(("leaf", "vec"), None),
        P(("leaf", "vec"), None, None),
        P("leaf", None, None),
        P("leaf", None, None, None),
        P("leaf", None),
        P("leaf"),
        P("leaf", None, None, None),
        P("leaf", None, None, None),
    )
    return jax.shard_map(
        local, mesh=mesh, in_specs=in_specs, out_specs=P("vec", "leaf"), check_vma=False
    )
```

```python
import functools

import jax
import jax.numpy as jnp
from jax import lax
from jax.experimental import pallas as pl
from jax.experimental.pallas import tpu as pltpu
from jax.sharding import PartitionSpec as P

MESH = pl.DeviceIdType.MESH
F32 = jnp.float32
BF16 = jnp.bfloat16
NN = (((1,), (0,)), ((), ()))
NT = (((1,), (1,)), ((), ()))
TN = (((0,), (0,)), ((), ()))
NX, NY, NZ = 4, 8, 8
LEVELS = 7
EARLY = 3


def dot(a, b, dims=NN):
    return lax.dot_general(a, b, dims, preferred_element_type=F32)


def drain(ref, sem):
    pltpu.make_async_copy(ref, ref, sem).wait()


def flipped(value, mask):
    out = 0
    for b in range(3):
        bit = lax.rem(value // (1 << b), 2)
        out = out + (1 << b) * ((1 - bit) if (mask >> b) & 1 else bit)
    return out


def twice(block):
    zero = jnp.zeros_like(block)
    return jnp.concatenate(
        [jnp.concatenate([block, zero], axis=1), jnp.concatenate([zero, block], axis=1)],
        axis=0,
    )


REACH = (0, 1, 2, 3, 4, 3, 2, 3)
FARTHEST_FIRST = sorted(range(1, NY * NZ), key=lambda d: -(REACH[d // NY] + REACH[d % NY]))


def kernel(
    vectors,
    near_blocks,
    near_list,
    bases,
    leaf_maps,
    far_blocks,
    far_list,
    far_count,
    level_maps,
    coupling,
    out,
    xs,
    own_x,
    x16,
    near_b,
    near_l,
    basis,
    maps,
    far_b,
    far_l,
    far_c,
    level_own,
    level_sib,
    coup,
    lift,
    lifts,
    weights,
    pair_coup,
    roots,
    coefs,
    terms,
    tree,
    local_out,
    result,
    parts,
    loc,
    send,
    recv,
    tree_recv,
    token,
):
    leaf = lax.axis_index("leaf")
    q = lax.axis_index("vec")
    core = lax.rem(leaf, 2)
    chip = leaf // 2
    y = lax.rem(chip, NY)
    z = chip // NY

    def leaf_at(zz, yy, cc):
        return (zz * NY + yy) * 2 + cc

    sib = leaf_at(z, y, 1 - core)
    off_chip = leaf - 1 + 2 * core
    off_slot = 32 - 32 * core
    has_off = jnp.logical_and(leaf > 0, leaf < 2 * NY * NZ - 1)
    x_peers = [lax.rem(q + d, NX) for d in (1, 2, 3)]
    by_root = [(leaf, p) for p in x_peers] + [(sib, lax.rem(q + d, NX)) for d in range(4)]
    steps = (1, 2, NY - 2, NY - 1)
    close = [(leaf_at(z, lax.rem(y + d, NY), core), q) for d in steps]
    inside = [
        (z >= 2, (leaf_at(z - 2, y, core), q)),
        (z >= 1, (leaf_at(z - 1, y, core), q)),
        (z < NZ - 1, (leaf_at(z + 1, y, core), q)),
        (z < NZ - 2, (leaf_at(z + 2, y, core), q)),
        (has_off, (off_chip, q)),
    ]
    n_close = len(close) + sum(jnp.where(ok, 1, 0) for ok, _ in inside)
    opposite = (leaf_at(lax.rem(z + NZ // 2, NZ), y, core), q)
    early = z < EARLY
    late = jnp.logical_not(early)
    row = [(leaf_at(z, lax.rem(y + d, NY), core), q) for d in range(1, NY)]

    barrier = pltpu.get_barrier_semaphore()

    def greet(sem, devs):
        for dev in devs:
            pl.semaphore_signal(sem, inc=1, device_id=dev, device_id_type=MESH)

    def greet_close(sem):
        greet(sem, close)
        for ok, dev in inside:
            pl.when(ok)(functools.partial(greet, sem, [dev]))

    greet(barrier, by_root)
    greet_close(barrier)

    copies = []

    def load(src, dst):
        c = pltpu.make_async_copy(src, dst, loc.at[len(copies)])
        c.start()
        copies.append(c)
        return c

    l_basis = load(bases, basis)
    l_maps = load(leaf_maps.at[pl.ds(q * 8, 8)], maps)
    for g in range(4):
        pltpu.make_async_copy(
            vectors.at[:, pl.ds(g * 2048, 2048)], xs.at[q * 4 + g], loc.at[15]
        ).start()
    l_level = load(level_maps.at[0], level_own)
    l_coup = load(coupling.at[0], coup)
    l_nl = load(near_list, near_l)
    l_fl = load(far_list, far_l)
    l_fc = load(far_count, far_c)
    l_near = load(near_blocks, near_b)
    l_far = load(far_blocks.at[pl.ds(q * 8, 8)], far_b)

    pl.semaphore_wait(barrier, len(by_root) + n_close)

    def push(src, dst, k, dev, rsem=None):
        pltpu.make_async_remote_copy(
            src_ref=src,
            dst_ref=dst,
            send_sem=send.at[k],
            recv_sem=recv.at[k] if rsem is None else rsem,
            device_id=dev,
            device_id_type=MESH,
        ).start()

    def chunk(g):
        return xs.at[q * 4 + g]

    drain(xs.at[pl.ds(0, 4)], loc.at[15])
    for p in x_peers:
        push(chunk(p), xs.at[q * 4 + p], 0, (leaf, p))
    push(level_maps.at[0], level_sib, 1, (sib, q))
    greet_close(token.at[0])

    l_basis.wait()
    l_maps.wait()
    for i in range(8):
        block = dot(maps[i], basis[i], TN).astype(BF16)
        lift[0:64, i * 256 : (i + 1) * 256] = block
        lift[64:128, i * 256 : (i + 1) * 256] = block
        lifts[q, :, i * 256 : (i + 1) * 256] = block
    l_level.wait()
    weights[0:128, 0:128] = jnp.zeros((128, 128), BF16)
    for t in range(1, LEVELS):
        weights[0:128, t * 128 : (t + 1) * 128] = twice(level_own[t])
    l_coup.wait()
    for t in range(LEVELS):
        pair_coup[t] = twice(coup[t])
    drain(level_sib, recv.at[1])
    for t in range(LEVELS):
        weights[128:256, t * 128 : (t + 1) * 128] = twice(level_sib[t])

    def block_of(g):
        parts = [xs[s * 4 + g].astype(F32) for s in range(4)]
        return jnp.concatenate(parts, axis=0).astype(BF16)

    def hear_close():
        pl.semaphore_wait(token.at[0], n_close)
        greet(token.at[1], [opposite])

    pl.when(late)(hear_close)
    low = lax.broadcasted_iota(jnp.int32, (8, 128), 1) < 64

    drain(xs.at[pl.ds(0, 3)], recv.at[0])
    own = block_of(q)
    part = dot(own, lift[...], NT)
    roots[q] = jnp.where(low, part[0:8], part[8:16])
    for dev in by_root[:3]:
        push(roots.at[q], roots.at[q], 3, dev)
    for dev in by_root[3:]:
        push(roots.at[q], roots.at[4 + q], 3, dev)
    for d in (1, 2, 3):
        for p in x_peers:
            g = lax.rem(p + d, NX)
            push(chunk(g), xs.at[q * 4 + g], 2, (leaf, p))

    own_x[...] = own
    mine = 16 + q * 4
    for i in range(4):
        two = [
            dot(own_x[:, l * 256 : (l + 1) * 256], basis[l], NT) for l in (2 * i, 2 * i + 1)
        ]
        coefs[mine + i] = jnp.concatenate(two, axis=1).astype(BF16)

    pl.when(early)(hear_close)
    src = coefs.at[pl.ds(mine, 4)]
    for dev in by_root[:3]:
        push(src, src, 4, dev)
    for dev in by_root[3:]:
        push(src, coefs.at[pl.ds(32 - off_slot + q * 4, 4)], 4, dev)

    @pl.when(has_off)
    def _():
        for d in range(4):
            push(src, coefs.at[pl.ds(off_slot + q * 4, 4)], 8, (off_chip, lax.rem(q + d, NX)))

    @pl.when(jnp.logical_not(has_off))
    def _():
        coefs[pl.ds(32 * core, 16)] = jnp.zeros((16, 16, 128), BF16)

    right, left = lax.rem(q + 1, NX), lax.rem(q + 3, NX)

    def share_lift():
        push(lifts.at[q], lifts.at[q], 6, (leaf, right))
        push(lifts.at[q], lifts.at[q], 9, (leaf, left))

    def pass_lift():
        drain(lifts.at[0], recv.at[6])
        one = lifts.at[left, pl.ds(0, 32)]
        push(one, one, 10, (leaf, right))
        drain(lifts.at[0], recv.at[9])
        two = lifts.at[right, pl.ds(32, 32)]
        push(two, two, 11, (leaf, left))

    def near_part():
        drain(xs.at[pl.ds(0, 9)], recv.at[2])
        for g in range(4):
            group = block_of(g)
            for i in range(8):
                x16[g * 8 + i] = group[:, i * 256 : (i + 1) * 256]
        l_nl.wait()
        l_near.wait()
        for i in range(8):
            total = None
            for n in range(2):
                at = jnp.clip(near_l[n, i] - leaf * 32, 0, 31)
                one = dot(x16[at], near_b[i, n], NT)
                total = one if total is None else total + one
            local_out[:, i * 256 : (i + 1) * 256] = total

    pl.when(early)(share_lift)
    pl.semaphore_wait(token.at[1], 1)
    greet(token.at[2], row)

    drain(roots.at[pl.ds(0, 7)], recv.at[3])
    root_own = (roots[0] + roots[1]) + (roots[2] + roots[3])
    root_sib = (roots[4] + roots[5]) + (roots[6] + roots[7])
    both = jnp.concatenate([root_own, root_sib], axis=1).astype(BF16)
    sums = dot(both, weights[...])
    for t in range(1, LEVELS):
        term = sums[:, t * 128 : (t + 1) * 128] * (2.0 ** (-0.5 * t))
        terms[t - 1] = term.astype(BF16)
    pl.semaphore_wait(token.at[2], len(row))
    for d in FARTHEST_FIRST:
        t = d.bit_length()
        dev = (leaf_at(flipped(z, d // NY), flipped(y, d % NY), core), q)
        push(terms.at[t - 1], tree.at[d], 5, dev, tree_recv.at[t - 1])

    coupled = dot(sums[:, 0:128].astype(BF16), pair_coup[0], NT)
    pl.when(early)(pass_lift)
    near_part()
    l_fl.wait()
    l_fc.wait()
    l_far.wait()
    drain(coefs.at[pl.ds(0, 28)], recv.at[4])

    @pl.when(has_off)
    def _():
        drain(coefs.at[pl.ds(0, 16)], recv.at[8])

    for i in range(8):
        total = None
        for f in range(6):
            at = jnp.clip(far_l[f, q * 8 + i] - leaf * 32 + 32, 0, 95)
            pair = coefs[at // 2].astype(F32)
            odd = jnp.full((16, 64), lax.rem(at, 2), jnp.int32) == 1
            used = jnp.full((16, 64), far_c[q * 8 + i], jnp.int32) > f
            value = jnp.where(odd, pair[:, 64:], pair[:, :64])
            value = jnp.where(used, value, 0.0).astype(BF16)
            one = dot(value, far_b[i, f], NT)
            total = one if total is None else total + one
        local_out[:, i * 256 : (i + 1) * 256] += dot(total.astype(BF16), basis[i])

    def give_back(total, cols):
        for p in range(4):
            result[p, :, cols] = total[4 * p : 4 * p + 4].astype(BF16)
        for p in x_peers:
            push(result.at[p, :, cols], parts.at[q, :, cols], 7, (leaf, p))

    halves = (slice(0, 1024), slice(1024, 2048))

    @pl.when(early)
    def _():
        for cols in halves:
            give_back(local_out[:, cols], cols)
        parts[q] = result[q]

    for t in range(1, LEVELS):
        lo, hi = 1 << (t - 1), 1 << t
        drain(tree.at[pl.ds(lo, hi - lo)], tree_recv.at[t - 1])
        blocks = [tree[d].astype(F32) for d in range(lo, hi)]
        while len(blocks) > 1:
            blocks = [a + b for a, b in zip(blocks[0::2], blocks[1::2])]
        coupled = coupled + dot(blocks[0].astype(BF16), pair_coup[t], NT)

    @pl.when(early)
    def _():
        right = jnp.full((8, 64), q, jnp.int32) < 2
        half = jnp.where(right, coupled[:, :64], coupled[:, 64:])
        turned = jnp.concatenate([half[4:8], half[0:4]], axis=0)
        odd = jnp.full((8, 64), lax.rem(q, 2), jnp.int32) == 1
        mine4 = jnp.where(odd, turned, half).astype(BF16)
        drain(lifts.at[0, pl.ds(0, 32)], recv.at[10])
        drain(lifts.at[0, pl.ds(0, 32)], recv.at[11])
        drain(parts.at[pl.ds(0, 3)], recv.at[7])
        for g in range(4):
            up_part = dot(mine4, lifts[g])
            out[:, g * 2048 : (g + 1) * 2048] = up_part[0:4] + parts[g].astype(F32)
        drain(lifts.at[0], send.at[6])
        drain(lifts.at[0], send.at[9])
        drain(lifts.at[0, pl.ds(0, 32)], send.at[10])
        drain(lifts.at[0, pl.ds(0, 32)], send.at[11])

    @pl.when(late)
    def _():
        spread = jnp.concatenate(
            [jnp.where(low, coupled, 0.0), jnp.where(low, 0.0, coupled)], axis=0
        ).astype(BF16)
        for cols in halves:
            give_back(dot(spread, lift[:, cols]) + local_out[:, cols], cols)
        parts[q] = result[q]
        drain(parts.at[pl.ds(0, 3)], recv.at[7])
        for g in range(4):
            out[:, g * 2048 : (g + 1) * 2048] = parts[g].astype(F32)

    drain(xs.at[pl.ds(0, 3)], send.at[0])
    drain(level_sib, send.at[1])
    drain(xs.at[pl.ds(0, 9)], send.at[2])
    drain(roots.at[pl.ds(0, 7)], send.at[3])
    drain(coefs.at[pl.ds(0, 28)], send.at[4])

    @pl.when(has_off)
    def _():
        drain(coefs.at[pl.ds(0, 16)], send.at[8])

    drain(tree.at[pl.ds(1, NY * NZ - 1)], send.at[5])
    drain(parts.at[pl.ds(0, 3)], send.at[7])


def local(
    vectors,
    near_blocks,
    near_list,
    bases,
    leaf_maps,
    far_blocks,
    far_list,
    far_count,
    level_maps,
    coupling,
):
    operands = (
        vectors,
        near_blocks,
        near_list.T,
        bases.transpose(0, 2, 1),
        leaf_maps,
        far_blocks,
        far_list.T,
        far_count,
        level_maps,
        coupling,
    )
    return pl.pallas_call(
        kernel,
        out_shape=pltpu.VMEM((4, 8192), F32),
        in_specs=[pl.BlockSpec(memory_space=pl.ANY)] * 10,
        out_specs=pl.BlockSpec(memory_space=pltpu.VMEM),
        scratch_shapes=[
            pltpu.VMEM((16, 4, 2048), BF16),
            pltpu.VMEM((16, 2048), BF16),
            pltpu.VMEM((32, 16, 256), BF16),
            pltpu.VMEM((8, 2, 256, 256), BF16),
            pltpu.SMEM((2, 8), jnp.int32),
            pltpu.VMEM((8, 64, 256), BF16),
            pltpu.VMEM((8, 64, 64), BF16),
            pltpu.VMEM((8, 6, 64, 64), BF16),
            pltpu.SMEM((6, 32), jnp.int32),
            pltpu.SMEM((32,), jnp.int32),
            pltpu.VMEM((LEVELS, 64, 64), BF16),
            pltpu.VMEM((LEVELS, 64, 64), BF16),
            pltpu.VMEM((LEVELS, 64, 64), BF16),
            pltpu.VMEM((128, 2048), BF16),
            pltpu.VMEM((4, 64, 2048), BF16),
            pltpu.VMEM((256, LEVELS * 128), BF16),
            pltpu.VMEM((LEVELS, 128, 128), BF16),
            pltpu.VMEM((8, 8, 128), F32),
            pltpu.VMEM((48, 16, 128), BF16),
            pltpu.VMEM((LEVELS - 1, 8, 128), BF16),
            pltpu.VMEM((NY * NZ, 8, 128), BF16),
            pltpu.VMEM((16, 2048), F32),
            pltpu.VMEM((4, 4, 2048), BF16),
            pltpu.VMEM((4, 4, 2048), BF16),
            pltpu.SemaphoreType.DMA((16,)),
            pltpu.SemaphoreType.DMA((12,)),
            pltpu.SemaphoreType.DMA((12,)),
            pltpu.SemaphoreType.DMA((LEVELS - 1,)),
            pltpu.SemaphoreType.REGULAR((3,)),
        ],
        compiler_params=pltpu.CompilerParams(
            collective_id=0, has_side_effects=True, vmem_limit_bytes=48 * 2**20
        ),
        name="h2_product",
    )(*(pltpu.with_memory_space_constraint(a, pltpu.HBM) for a in operands))


def solution(mesh):
    in_specs = (
        P("vec", "leaf"),
        P(("leaf", "vec"), None, None, None),
        P(("leaf", "vec"), None),
        P(("leaf", "vec"), None, None),
        P("leaf", None, None),
        P("leaf", None, None, None),
        P("leaf", None),
        P("leaf"),
        P("leaf", None, None, None),
        P("leaf", None, None, None),
    )
    return jax.shard_map(
        local, mesh=mesh, in_specs=in_specs, out_specs=P("vec", "leaf"), check_vma=False
    )
```

```python
import functools

import jax
import jax.numpy as jnp
from jax import lax
from jax.experimental import pallas as pl
from jax.experimental.pallas import tpu as pltpu
from jax.sharding import PartitionSpec as P

MESH = pl.DeviceIdType.MESH
F32 = jnp.float32
BF16 = jnp.bfloat16
NN = (((1,), (0,)), ((), ()))
NT = (((1,), (1,)), ((), ()))
TN = (((0,), (0,)), ((), ()))
NX, NY, NZ = 4, 8, 8
LEVELS = 7
EARLY = 3
SOON = 4


def dot(a, b, dims=NN):
    return lax.dot_general(a, b, dims, preferred_element_type=F32)


def drain(ref, sem):
    pltpu.make_async_copy(ref, ref, sem).wait()


def flipped(value, mask):
    out = 0
    for b in range(3):
        bit = lax.rem(value // (1 << b), 2)
        out = out + (1 << b) * ((1 - bit) if (mask >> b) & 1 else bit)
    return out


def twice(block):
    zero = jnp.zeros_like(block)
    return jnp.concatenate(
        [jnp.concatenate([block, zero], axis=1), jnp.concatenate([zero, block], axis=1)],
        axis=0,
    )


REACH = (0, 1, 2, 3, 4, 3, 2, 3)
FARTHEST_FIRST = sorted(range(1, NY * NZ), key=lambda d: -(REACH[d // NY] + REACH[d % NY]))


def kernel(
    vectors,
    near_blocks,
    near_list,
    bases,
    leaf_maps,
    far_blocks,
    far_list,
    far_count,
    level_maps,
    coupling,
    out,
    xs,
    own_x,
    x16,
    near_b,
    near_l,
    basis,
    maps,
    far_b,
    far_l,
    far_c,
    level_own,
    level_sib,
    coup,
    lift,
    lifts,
    weights,
    pair_coup,
    roots,
    coefs,
    terms,
    tree,
    local_out,
    result,
    parts,
    loc,
    send,
    recv,
    tree_recv,
    token,
):
    leaf = lax.axis_index("leaf")
    q = lax.axis_index("vec")
    core = lax.rem(leaf, 2)
    chip = leaf // 2
    y = lax.rem(chip, NY)
    z = chip // NY

    def leaf_at(zz, yy, cc):
        return (zz * NY + yy) * 2 + cc

    sib = leaf_at(z, y, 1 - core)
    off_chip = leaf - 1 + 2 * core
    off_slot = 32 - 32 * core
    has_off = jnp.logical_and(leaf > 0, leaf < 2 * NY * NZ - 1)
    x_peers = [lax.rem(q + d, NX) for d in (2, 1, 3)]
    by_root = [(leaf, p) for p in x_peers] + [(sib, p) for p in x_peers + [q]]
    steps = (1, 2, NY - 2, NY - 1)
    close = [(leaf_at(z, lax.rem(y + d, NY), core), q) for d in steps]
    inside = [
        (z >= 2, (leaf_at(z - 2, y, core), q)),
        (z >= 1, (leaf_at(z - 1, y, core), q)),
        (z < NZ - 1, (leaf_at(z + 1, y, core), q)),
        (z < NZ - 2, (leaf_at(z + 2, y, core), q)),
        (has_off, (off_chip, q)),
    ]
    n_close = len(close) + sum(jnp.where(ok, 1, 0) for ok, _ in inside)
    opposite = (leaf_at(lax.rem(z + NZ // 2, NZ), y, core), q)
    early = z < EARLY
    late = jnp.logical_not(early)
    soon = z < SOON
    row = [(leaf_at(z, lax.rem(y + d, NY), core), q) for d in range(1, NY)]

    barrier = pltpu.get_barrier_semaphore()

    def greet(sem, devs):
        for dev in devs:
            pl.semaphore_signal(sem, inc=1, device_id=dev, device_id_type=MESH)

    def greet_close(sem):
        greet(sem, close)
        for ok, dev in inside:
            pl.when(ok)(functools.partial(greet, sem, [dev]))

    greet(barrier, by_root)
    greet_close(barrier)

    copies = []

    def load(src, dst):
        c = pltpu.make_async_copy(src, dst, loc.at[len(copies)])
        c.start()
        copies.append(c)
        return c

    l_basis = load(bases, basis)
    l_maps = load(leaf_maps.at[pl.ds(q * 8, 8)], maps)
    for g in range(4):
        pltpu.make_async_copy(
            vectors.at[:, pl.ds(g * 2048, 2048)], xs.at[q * 4 + g], loc.at[15]
        ).start()
    l_level = load(level_maps.at[0], level_own)
    l_coup = load(coupling.at[0], coup)
    l_nl = load(near_list, near_l)
    l_fl = load(far_list, far_l)
    l_fc = load(far_count, far_c)
    l_near = load(near_blocks, near_b)
    l_far = load(far_blocks.at[pl.ds(q * 8, 8)], far_b)

    pl.semaphore_wait(barrier, len(by_root) + n_close)

    def push(src, dst, k, dev, rsem=None):
        pltpu.make_async_remote_copy(
            src_ref=src,
            dst_ref=dst,
            send_sem=send.at[k],
            recv_sem=recv.at[k] if rsem is None else rsem,
            device_id=dev,
            device_id_type=MESH,
        ).start()

    def chunk(g):
        return xs.at[q * 4 + g]

    drain(xs.at[pl.ds(0, 4)], loc.at[15])
    for p in x_peers:
        push(chunk(p), xs.at[q * 4 + p], 0, (leaf, p))
    push(level_maps.at[0], level_sib, 1, (sib, q))
    greet_close(token.at[0])

    l_basis.wait()
    l_maps.wait()
    for i in range(8):
        block = dot(maps[i], basis[i], TN).astype(BF16)
        lift[0:64, i * 256 : (i + 1) * 256] = block
        lift[64:128, i * 256 : (i + 1) * 256] = block
        lifts[q, :, i * 256 : (i + 1) * 256] = block
    l_level.wait()
    weights[0:128, 0:128] = jnp.zeros((128, 128), BF16)
    for t in range(1, LEVELS):
        weights[0:128, t * 128 : (t + 1) * 128] = twice(level_own[t])
    l_coup.wait()
    for t in range(LEVELS):
        pair_coup[t] = twice(coup[t])
    drain(level_sib, recv.at[1])
    for t in range(LEVELS):
        weights[128:256, t * 128 : (t + 1) * 128] = twice(level_sib[t])

    def block_of(g):
        parts = [xs[s * 4 + g].astype(F32) for s in range(4)]
        return jnp.concatenate(parts, axis=0).astype(BF16)

    def hear_close():
        pl.semaphore_wait(token.at[0], n_close)
        greet(token.at[1], [opposite])

    pl.when(late)(hear_close)
    low = lax.broadcasted_iota(jnp.int32, (8, 128), 1) < 64

    drain(xs.at[pl.ds(0, 3)], recv.at[0])
    own = block_of(q)
    part = dot(own, lift[...], NT)
    roots[q] = jnp.where(low, part[0:8], part[8:16])
    for dev in by_root[:3]:
        push(roots.at[q], roots.at[q], 3, dev)
    for dev in by_root[3:]:
        push(roots.at[q], roots.at[4 + q], 3, dev)
    def share_rest():
        for d in (1, 2, 3):
            for p in x_peers:
                g = lax.rem(p + d, NX)
                push(chunk(g), xs.at[q * 4 + g], 2, (leaf, p))

    pl.when(soon)(share_rest)

    own_x[...] = own
    mine = 16 + q * 4
    for i in range(4):
        two = [
            dot(own_x[:, l * 256 : (l + 1) * 256], basis[l], NT) for l in (2 * i, 2 * i + 1)
        ]
        coefs[mine + i] = jnp.concatenate(two, axis=1).astype(BF16)

    pl.when(early)(hear_close)
    src = coefs.at[pl.ds(mine, 4)]
    def share_coefs():
        for dev in by_root[:3]:
            push(src, src, 4, dev)
        for dev in by_root[3:]:
            push(src, coefs.at[pl.ds(32 - off_slot + q * 4, 4)], 4, dev)

        @pl.when(has_off)
        def _():
            for d in range(4):
                push(src, coefs.at[pl.ds(off_slot + q * 4, 4)], 8, (off_chip, lax.rem(q + d, NX)))

    pl.when(soon)(share_coefs)

    @pl.when(jnp.logical_not(has_off))
    def _():
        coefs[pl.ds(32 * core, 16)] = jnp.zeros((16, 16, 128), BF16)

    right, left = lax.rem(q + 1, NX), lax.rem(q + 3, NX)

    def share_lift():
        push(lifts.at[q], lifts.at[q], 6, (leaf, right))
        push(lifts.at[q], lifts.at[q], 9, (leaf, left))

    def pass_lift():
        drain(lifts.at[0], recv.at[6])
        one = lifts.at[left, pl.ds(0, 32)]
        push(one, one, 10, (leaf, right))
        drain(lifts.at[0], recv.at[9])
        two = lifts.at[right, pl.ds(32, 32)]
        push(two, two, 11, (leaf, left))

    def near_part():
        drain(xs.at[pl.ds(0, 9)], recv.at[2])
        for g in range(4):
            group = block_of(g)
            for i in range(8):
                x16[g * 8 + i] = group[:, i * 256 : (i + 1) * 256]
        l_nl.wait()
        l_near.wait()
        for i in range(8):
            total = None
            for n in range(2):
                at = jnp.clip(near_l[n, i] - leaf * 32, 0, 31)
                one = dot(x16[at], near_b[i, n], NT)
                total = one if total is None else total + one
            local_out[:, i * 256 : (i + 1) * 256] = total

    pl.when(early)(share_lift)
    pl.semaphore_wait(token.at[1], 1)
    greet(token.at[2], row)

    drain(roots.at[pl.ds(0, 7)], recv.at[3])
    root_own = (roots[0] + roots[1]) + (roots[2] + roots[3])
    root_sib = (roots[4] + roots[5]) + (roots[6] + roots[7])
    both = jnp.concatenate([root_own, root_sib], axis=1).astype(BF16)

    def send_terms(levels):
        first, width = levels[0] * 128, len(levels) * 128
        sums = dot(both, weights[:, first : first + width])
        for i, t in enumerate(levels):
            if t > 0:
                term = sums[:, i * 128 : (i + 1) * 128] * (2.0 ** (-0.5 * t))
                terms[t - 1] = term.astype(BF16)
        if levels[-1] == LEVELS - 1:
            pl.semaphore_wait(token.at[2], len(row))
        for d in FARTHEST_FIRST:
            t = d.bit_length()
            if t in levels:
                dev = (leaf_at(flipped(z, d // NY), flipped(y, d % NY), core), q)
                push(terms.at[t - 1], tree.at[d], 5, dev, tree_recv.at[t - 1])
        return sums

    send_terms([LEVELS - 1])
    sums = send_terms(list(range(LEVELS - 1)))

    @pl.when(jnp.logical_not(soon))
    def _():
        share_rest()
        share_coefs()

    coupled = dot(sums[:, 0:128].astype(BF16), pair_coup[0], NT)
    pl.when(early)(pass_lift)
    near_part()
    l_fl.wait()
    l_fc.wait()
    l_far.wait()
    drain(coefs.at[pl.ds(0, 28)], recv.at[4])

    @pl.when(has_off)
    def _():
        drain(coefs.at[pl.ds(0, 16)], recv.at[8])

    for i in range(8):
        total = None
        for f in range(6):
            at = jnp.clip(far_l[f, q * 8 + i] - leaf * 32 + 32, 0, 95)
            pair = coefs[at // 2].astype(F32)
            odd = jnp.full((16, 64), lax.rem(at, 2), jnp.int32) == 1
            used = jnp.full((16, 64), far_c[q * 8 + i], jnp.int32) > f
            value = jnp.where(odd, pair[:, 64:], pair[:, :64])
            value = jnp.where(used, value, 0.0).astype(BF16)
            one = dot(value, far_b[i, f], NT)
            total = one if total is None else total + one
        local_out[:, i * 256 : (i + 1) * 256] += dot(total.astype(BF16), basis[i])

    def give_back(total, cols):
        for p in range(4):
            result[p, :, cols] = total[4 * p : 4 * p + 4].astype(BF16)
        for p in x_peers:
            push(result.at[p, :, cols], parts.at[q, :, cols], 7, (leaf, p))

    halves = (slice(0, 1024), slice(1024, 2048))

    @pl.when(early)
    def _():
        for cols in halves:
            give_back(local_out[:, cols], cols)
        parts[q] = result[q]

    for t in range(1, LEVELS):
        lo, hi = 1 << (t - 1), 1 << t
        drain(tree.at[pl.ds(lo, hi - lo)], tree_recv.at[t - 1])
        blocks = [tree[d].astype(F32) for d in range(lo, hi)]
        while len(blocks) > 1:
            blocks = [a + b for a, b in zip(blocks[0::2], blocks[1::2])]
        coupled = coupled + dot(blocks[0].astype(BF16), pair_coup[t], NT)

    @pl.when(early)
    def _():
        right = jnp.full((8, 64), q, jnp.int32) < 2
        half = jnp.where(right, coupled[:, :64], coupled[:, 64:])
        turned = jnp.concatenate([half[4:8], half[0:4]], axis=0)
        odd = jnp.full((8, 64), lax.rem(q, 2), jnp.int32) == 1
        mine4 = jnp.where(odd, turned, half).astype(BF16)
        drain(lifts.at[0, pl.ds(0, 32)], recv.at[10])
        drain(lifts.at[0, pl.ds(0, 32)], recv.at[11])
        drain(parts.at[pl.ds(0, 3)], recv.at[7])
        for g in range(4):
            up_part = dot(mine4, lifts[g])
            out[:, g * 2048 : (g + 1) * 2048] = up_part[0:4] + parts[g].astype(F32)
        drain(lifts.at[0], send.at[6])
        drain(lifts.at[0], send.at[9])
        drain(lifts.at[0, pl.ds(0, 32)], send.at[10])
        drain(lifts.at[0, pl.ds(0, 32)], send.at[11])

    @pl.when(late)
    def _():
        spread = jnp.concatenate(
            [jnp.where(low, coupled, 0.0), jnp.where(low, 0.0, coupled)], axis=0
        ).astype(BF16)
        for cols in halves:
            give_back(dot(spread, lift[:, cols]) + local_out[:, cols], cols)
        parts[q] = result[q]
        drain(parts.at[pl.ds(0, 3)], recv.at[7])
        for g in range(4):
            out[:, g * 2048 : (g + 1) * 2048] = parts[g].astype(F32)

    drain(xs.at[pl.ds(0, 3)], send.at[0])
    drain(level_sib, send.at[1])
    drain(xs.at[pl.ds(0, 9)], send.at[2])
    drain(roots.at[pl.ds(0, 7)], send.at[3])
    drain(coefs.at[pl.ds(0, 28)], send.at[4])

    @pl.when(has_off)
    def _():
        drain(coefs.at[pl.ds(0, 16)], send.at[8])

    drain(tree.at[pl.ds(1, NY * NZ - 1)], send.at[5])
    drain(parts.at[pl.ds(0, 3)], send.at[7])


def local(
    vectors,
    near_blocks,
    near_list,
    bases,
    leaf_maps,
    far_blocks,
    far_list,
    far_count,
    level_maps,
    coupling,
):
    operands = (
        vectors,
        near_blocks,
        near_list.T,
        bases.transpose(0, 2, 1),
        leaf_maps,
        far_blocks,
        far_list.T,
        far_count,
        level_maps,
        coupling,
    )
    return pl.pallas_call(
        kernel,
        out_shape=pltpu.VMEM((4, 8192), F32),
        in_specs=[pl.BlockSpec(memory_space=pl.ANY)] * 10,
        out_specs=pl.BlockSpec(memory_space=pltpu.VMEM),
        scratch_shapes=[
            pltpu.VMEM((16, 4, 2048), BF16),
            pltpu.VMEM((16, 2048), BF16),
            pltpu.VMEM((32, 16, 256), BF16),
            pltpu.VMEM((8, 2, 256, 256), BF16),
            pltpu.SMEM((2, 8), jnp.int32),
            pltpu.VMEM((8, 64, 256), BF16),
            pltpu.VMEM((8, 64, 64), BF16),
            pltpu.VMEM((8, 6, 64, 64), BF16),
            pltpu.SMEM((6, 32), jnp.int32),
            pltpu.SMEM((32,), jnp.int32),
            pltpu.VMEM((LEVELS, 64, 64), BF16),
            pltpu.VMEM((LEVELS, 64, 64), BF16),
            pltpu.VMEM((LEVELS, 64, 64), BF16),
            pltpu.VMEM((128, 2048), BF16),
            pltpu.VMEM((4, 64, 2048), BF16),
            pltpu.VMEM((256, LEVELS * 128), BF16),
            pltpu.VMEM((LEVELS, 128, 128), BF16),
            pltpu.VMEM((8, 8, 128), F32),
            pltpu.VMEM((48, 16, 128), BF16),
            pltpu.VMEM((LEVELS - 1, 8, 128), BF16),
            pltpu.VMEM((NY * NZ, 8, 128), BF16),
            pltpu.VMEM((16, 2048), F32),
            pltpu.VMEM((4, 4, 2048), BF16),
            pltpu.VMEM((4, 4, 2048), BF16),
            pltpu.SemaphoreType.DMA((16,)),
            pltpu.SemaphoreType.DMA((12,)),
            pltpu.SemaphoreType.DMA((12,)),
            pltpu.SemaphoreType.DMA((LEVELS - 1,)),
            pltpu.SemaphoreType.REGULAR((3,)),
        ],
        compiler_params=pltpu.CompilerParams(
            collective_id=0, has_side_effects=True, vmem_limit_bytes=48 * 2**20
        ),
        name="h2_product",
    )(*(pltpu.with_memory_space_constraint(a, pltpu.HBM) for a in operands))


def solution(mesh):
    in_specs = (
        P("vec", "leaf"),
        P(("leaf", "vec"), None, None, None),
        P(("leaf", "vec"), None),
        P(("leaf", "vec"), None, None),
        P("leaf", None, None),
        P("leaf", None, None, None),
        P("leaf", None),
        P("leaf"),
        P("leaf", None, None, None),
        P("leaf", None, None, None),
    )
    return jax.shard_map(
        local, mesh=mesh, in_specs=in_specs, out_specs=P("vec", "leaf"), check_vma=False
    )
```

```python
import functools

import jax
import jax.numpy as jnp
from jax import lax
from jax.experimental import pallas as pl
from jax.experimental.pallas import tpu as pltpu
from jax.sharding import PartitionSpec as P

MESH = pl.DeviceIdType.MESH
F32 = jnp.float32
BF16 = jnp.bfloat16
NN = (((1,), (0,)), ((), ()))
NT = (((1,), (1,)), ((), ()))
TN = (((0,), (0,)), ((), ()))
NX, NY, NZ = 4, 8, 8
LEVELS = 7
EARLY = 3
SOON = 4


def dot(a, b, dims=NN):
    return lax.dot_general(a, b, dims, preferred_element_type=F32)


def drain(ref, sem):
    pltpu.make_async_copy(ref, ref, sem).wait()


def flipped(value, mask):
    out = 0
    for b in range(3):
        bit = lax.rem(value // (1 << b), 2)
        out = out + (1 << b) * ((1 - bit) if (mask >> b) & 1 else bit)
    return out


def twice(block):
    zero = jnp.zeros_like(block)
    return jnp.concatenate(
        [jnp.concatenate([block, zero], axis=1), jnp.concatenate([zero, block], axis=1)],
        axis=0,
    )


REACH = (0, 1, 2, 3, 4, 3, 2, 3)
FARTHEST_FIRST = sorted(range(1, NY * NZ), key=lambda d: -(REACH[d // NY] + REACH[d % NY]))


def kernel(
    vectors,
    near_blocks,
    near_list,
    bases,
    leaf_maps,
    far_blocks,
    far_list,
    far_count,
    level_maps,
    coupling,
    out,
    xs,
    own_x,
    x16,
    near_b,
    near_l,
    basis,
    maps,
    far_b,
    far_l,
    far_c,
    level_own,
    level_sib,
    coup,
    lift,
    lifts,
    weights,
    pair_coup,
    roots,
    coefs,
    terms,
    tree,
    local_out,
    result,
    parts,
    loc,
    send,
    recv,
    tree_recv,
    token,
):
    leaf = lax.axis_index("leaf")
    q = lax.axis_index("vec")
    core = lax.rem(leaf, 2)
    chip = leaf // 2
    y = lax.rem(chip, NY)
    z = chip // NY

    def leaf_at(zz, yy, cc):
        return (zz * NY + yy) * 2 + cc

    sib = leaf_at(z, y, 1 - core)
    off_chip = leaf - 1 + 2 * core
    off_slot = 32 - 32 * core
    has_off = jnp.logical_and(leaf > 0, leaf < 2 * NY * NZ - 1)
    x_peers = [lax.rem(q + d, NX) for d in (2, 1, 3)]
    by_root = [(leaf, p) for p in x_peers] + [(sib, p) for p in x_peers + [q]]
    steps = (1, 2, NY - 2, NY - 1)
    close = [(leaf_at(z, lax.rem(y + d, NY), core), q) for d in steps]
    inside = [
        (z >= 2, (leaf_at(z - 2, y, core), q)),
        (z >= 1, (leaf_at(z - 1, y, core), q)),
        (z < NZ - 1, (leaf_at(z + 1, y, core), q)),
        (z < NZ - 2, (leaf_at(z + 2, y, core), q)),
        (has_off, (off_chip, q)),
    ]
    n_close = len(close) + sum(jnp.where(ok, 1, 0) for ok, _ in inside)
    opposite = (leaf_at(lax.rem(z + NZ // 2, NZ), y, core), q)
    early = z < EARLY
    late = jnp.logical_not(early)
    soon = z < SOON
    row = [(leaf_at(z, lax.rem(y + d, NY), core), q) for d in range(1, NY)]

    barrier = pltpu.get_barrier_semaphore()

    def greet(sem, devs):
        for dev in devs:
            pl.semaphore_signal(sem, inc=1, device_id=dev, device_id_type=MESH)

    def greet_close(sem):
        greet(sem, close)
        for ok, dev in inside:
            pl.when(ok)(functools.partial(greet, sem, [dev]))

    greet(barrier, by_root)
    greet_close(barrier)

    copies = []

    def load(src, dst):
        c = pltpu.make_async_copy(src, dst, loc.at[len(copies)])
        c.start()
        copies.append(c)
        return c

    l_basis = load(bases, basis)
    l_maps = load(leaf_maps.at[pl.ds(q * 8, 8)], maps)
    for g in range(4):
        pltpu.make_async_copy(
            vectors.at[:, pl.ds(g * 2048, 2048)], xs.at[q * 4 + g], loc.at[15]
        ).start()
    l_level = load(level_maps.at[0], level_own)
    l_coup = load(coupling.at[0], coup)

    pl.semaphore_wait(barrier, len(by_root) + n_close)

    def push(src, dst, k, dev, rsem=None):
        pltpu.make_async_remote_copy(
            src_ref=src,
            dst_ref=dst,
            send_sem=send.at[k],
            recv_sem=recv.at[k] if rsem is None else rsem,
            device_id=dev,
            device_id_type=MESH,
        ).start()

    def chunk(g):
        return xs.at[q * 4 + g]

    drain(xs.at[pl.ds(0, 4)], loc.at[15])
    for p in x_peers:
        push(chunk(p), xs.at[q * 4 + p], 0, (leaf, p))
    push(level_maps.at[0], level_sib, 1, (sib, q))
    greet_close(token.at[0])
    l_nl = load(near_list, near_l)
    l_fl = load(far_list, far_l)
    l_fc = load(far_count, far_c)
    l_near = load(near_blocks, near_b)
    l_far = load(far_blocks.at[pl.ds(q * 8, 8)], far_b)

    l_basis.wait()
    l_maps.wait()
    for i in range(8):
        block = dot(maps[i], basis[i], TN).astype(BF16)
        lift[0:64, i * 256 : (i + 1) * 256] = block
        lift[64:128, i * 256 : (i + 1) * 256] = block
        lifts[q, :, i * 256 : (i + 1) * 256] = block
    l_level.wait()
    weights[0:128, 0:128] = jnp.zeros((128, 128), BF16)
    for t in range(1, LEVELS):
        weights[0:128, t * 128 : (t + 1) * 128] = twice(level_own[t])
    l_coup.wait()
    for t in range(LEVELS):
        pair_coup[t] = twice(coup[t])
    drain(level_sib, recv.at[1])
    for t in range(LEVELS):
        weights[128:256, t * 128 : (t + 1) * 128] = twice(level_sib[t])

    def block_of(g):
        parts = [xs[s * 4 + g].astype(F32) for s in range(4)]
        return jnp.concatenate(parts, axis=0).astype(BF16)

    def hear_close():
        pl.semaphore_wait(token.at[0], n_close)
        greet(token.at[1], [opposite])

    pl.when(late)(hear_close)
    low = lax.broadcasted_iota(jnp.int32, (8, 128), 1) < 64

    drain(xs.at[pl.ds(0, 3)], recv.at[0])
    own = block_of(q)
    part = dot(own, lift[...], NT)
    roots[q] = jnp.where(low, part[0:8], part[8:16])
    for dev in by_root[:3]:
        push(roots.at[q], roots.at[q], 3, dev)
    for dev in by_root[3:]:
        push(roots.at[q], roots.at[4 + q], 3, dev)
    def share_rest():
        for d in (1, 2, 3):
            for p in x_peers:
                g = lax.rem(p + d, NX)
                push(chunk(g), xs.at[q * 4 + g], 2, (leaf, p))

    pl.when(soon)(share_rest)

    own_x[...] = own
    mine = 16 + q * 4
    for i in range(4):
        two = [
            dot(own_x[:, l * 256 : (l + 1) * 256], basis[l], NT) for l in (2 * i, 2 * i + 1)
        ]
        coefs[mine + i] = jnp.concatenate(two, axis=1).astype(BF16)

    pl.when(early)(hear_close)
    src = coefs.at[pl.ds(mine, 4)]
    def share_coefs():
        for dev in by_root[:3]:
            push(src, src, 4, dev)
        for dev in by_root[3:]:
            push(src, coefs.at[pl.ds(32 - off_slot + q * 4, 4)], 4, dev)

        @pl.when(has_off)
        def _():
            for d in range(4):
                push(src, coefs.at[pl.ds(off_slot + q * 4, 4)], 8, (off_chip, lax.rem(q + d, NX)))

    pl.when(soon)(share_coefs)

    @pl.when(jnp.logical_not(has_off))
    def _():
        coefs[pl.ds(32 * core, 16)] = jnp.zeros((16, 16, 128), BF16)

    right, left = lax.rem(q + 1, NX), lax.rem(q + 3, NX)

    def share_lift():
        push(lifts.at[q], lifts.at[q], 6, (leaf, right))
        push(lifts.at[q], lifts.at[q], 9, (leaf, left))

    def pass_lift():
        drain(lifts.at[0], recv.at[6])
        one = lifts.at[left, pl.ds(0, 32)]
        push(one, one, 10, (leaf, right))
        drain(lifts.at[0], recv.at[9])
        two = lifts.at[right, pl.ds(32, 32)]
        push(two, two, 11, (leaf, left))

    def near_part():
        drain(xs.at[pl.ds(0, 9)], recv.at[2])
        for g in range(4):
            group = block_of(g)
            for i in range(8):
                x16[g * 8 + i] = group[:, i * 256 : (i + 1) * 256]
        l_nl.wait()
        l_near.wait()
        for i in range(8):
            total = None
            for n in range(2):
                at = jnp.clip(near_l[n, i] - leaf * 32, 0, 31)
                one = dot(x16[at], near_b[i, n], NT)
                total = one if total is None else total + one
            local_out[:, i * 256 : (i + 1) * 256] = total

    pl.when(early)(share_lift)
    pl.semaphore_wait(token.at[1], 1)
    greet(token.at[2], row)

    drain(roots.at[pl.ds(0, 7)], recv.at[3])
    root_own = (roots[0] + roots[1]) + (roots[2] + roots[3])
    root_sib = (roots[4] + roots[5]) + (roots[6] + roots[7])
    both = jnp.concatenate([root_own, root_sib], axis=1).astype(BF16)

    def send_terms(levels):
        first, width = levels[0] * 128, len(levels) * 128
        sums = dot(both, weights[:, first : first + width])
        for i, t in enumerate(levels):
            if t > 0:
                term = sums[:, i * 128 : (i + 1) * 128] * (2.0 ** (-0.5 * t))
                terms[t - 1] = term.astype(BF16)
        if levels[-1] == LEVELS - 1:
            pl.semaphore_wait(token.at[2], len(row))
        for d in FARTHEST_FIRST:
            t = d.bit_length()
            if t in levels:
                dev = (leaf_at(flipped(z, d // NY), flipped(y, d % NY), core), q)
                push(terms.at[t - 1], tree.at[d], 5, dev, tree_recv.at[t - 1])
        return sums

    send_terms([LEVELS - 1])
    sums = send_terms(list(range(LEVELS - 1)))

    @pl.when(jnp.logical_not(soon))
    def _():
        share_rest()
        share_coefs()

    coupled = dot(sums[:, 0:128].astype(BF16), pair_coup[0], NT)
    pl.when(early)(pass_lift)
    near_part()
    l_fl.wait()
    l_fc.wait()
    l_far.wait()
    drain(coefs.at[pl.ds(0, 28)], recv.at[4])

    @pl.when(has_off)
    def _():
        drain(coefs.at[pl.ds(0, 16)], recv.at[8])

    for i in range(8):
        total = None
        for f in range(6):
            at = jnp.clip(far_l[f, q * 8 + i] - leaf * 32 + 32, 0, 95)
            pair = coefs[at // 2].astype(F32)
            odd = jnp.full((16, 64), lax.rem(at, 2), jnp.int32) == 1
            used = jnp.full((16, 64), far_c[q * 8 + i], jnp.int32) > f
            value = jnp.where(odd, pair[:, 64:], pair[:, :64])
            value = jnp.where(used, value, 0.0).astype(BF16)
            one = dot(value, far_b[i, f], NT)
            total = one if total is None else total + one
        local_out[:, i * 256 : (i + 1) * 256] += dot(total.astype(BF16), basis[i])

    def give_back(total, cols):
        for p in range(4):
            result[p, :, cols] = total[4 * p : 4 * p + 4].astype(BF16)
        for p in x_peers:
            push(result.at[p, :, cols], parts.at[q, :, cols], 7, (leaf, p))

    halves = (slice(0, 1024), slice(1024, 2048))

    @pl.when(early)
    def _():
        for cols in halves:
            give_back(local_out[:, cols], cols)
        parts[q] = result[q]

    for t in range(1, LEVELS):
        lo, hi = 1 << (t - 1), 1 << t
        if t == LEVELS - 1:
            drain(xs.at[pl.ds(0, 3)], send.at[0])
            drain(level_sib, send.at[1])
            drain(xs.at[pl.ds(0, 9)], send.at[2])
            drain(roots.at[pl.ds(0, 7)], send.at[3])
            drain(coefs.at[pl.ds(0, 28)], send.at[4])

            @pl.when(has_off)
            def _():
                drain(coefs.at[pl.ds(0, 16)], send.at[8])

            drain(tree.at[pl.ds(1, NY * NZ - 1)], send.at[5])

            @pl.when(early)
            def _():
                drain(lifts.at[0], send.at[6])
                drain(lifts.at[0], send.at[9])
                drain(lifts.at[0, pl.ds(0, 32)], send.at[10])
                drain(lifts.at[0, pl.ds(0, 32)], send.at[11])
                drain(lifts.at[0, pl.ds(0, 32)], recv.at[10])
                drain(lifts.at[0, pl.ds(0, 32)], recv.at[11])

        drain(tree.at[pl.ds(lo, hi - lo)], tree_recv.at[t - 1])
        blocks = [tree[d].astype(F32) for d in range(lo, hi)]
        while len(blocks) > 1:
            blocks = [a + b for a, b in zip(blocks[0::2], blocks[1::2])]
        coupled = coupled + dot(blocks[0].astype(BF16), pair_coup[t], NT)

    @pl.when(early)
    def _():
        right = jnp.full((8, 64), q, jnp.int32) < 2
        half = jnp.where(right, coupled[:, :64], coupled[:, 64:])
        turned = jnp.concatenate([half[4:8], half[0:4]], axis=0)
        odd = jnp.full((8, 64), lax.rem(q, 2), jnp.int32) == 1
        mine4 = jnp.where(odd, turned, half).astype(BF16)
        drain(parts.at[pl.ds(0, 3)], recv.at[7])
        for g in range(4):
            up_part = dot(mine4, lifts[g])
            out[:, g * 2048 : (g + 1) * 2048] = up_part[0:4] + parts[g].astype(F32)

    @pl.when(late)
    def _():
        spread = jnp.concatenate(
            [jnp.where(low, coupled, 0.0), jnp.where(low, 0.0, coupled)], axis=0
        ).astype(BF16)
        for cols in halves:
            give_back(dot(spread, lift[:, cols]) + local_out[:, cols], cols)
        parts[q] = result[q]
        drain(parts.at[pl.ds(0, 3)], recv.at[7])
        for g in range(4):
            out[:, g * 2048 : (g + 1) * 2048] = parts[g].astype(F32)
    drain(parts.at[pl.ds(0, 3)], send.at[7])


def local(
    vectors,
    near_blocks,
    near_list,
    bases,
    leaf_maps,
    far_blocks,
    far_list,
    far_count,
    level_maps,
    coupling,
):
    operands = (
        vectors,
        near_blocks,
        near_list.T,
        bases.transpose(0, 2, 1),
        leaf_maps,
        far_blocks,
        far_list.T,
        far_count,
        level_maps,
        coupling,
    )
    return pl.pallas_call(
        kernel,
        out_shape=pltpu.VMEM((4, 8192), F32),
        in_specs=[pl.BlockSpec(memory_space=pl.ANY)] * 10,
        out_specs=pl.BlockSpec(memory_space=pltpu.VMEM),
        scratch_shapes=[
            pltpu.VMEM((16, 4, 2048), BF16),
            pltpu.VMEM((16, 2048), BF16),
            pltpu.VMEM((32, 16, 256), BF16),
            pltpu.VMEM((8, 2, 256, 256), BF16),
            pltpu.SMEM((2, 8), jnp.int32),
            pltpu.VMEM((8, 64, 256), BF16),
            pltpu.VMEM((8, 64, 64), BF16),
            pltpu.VMEM((8, 6, 64, 64), BF16),
            pltpu.SMEM((6, 32), jnp.int32),
            pltpu.SMEM((32,), jnp.int32),
            pltpu.VMEM((LEVELS, 64, 64), BF16),
            pltpu.VMEM((LEVELS, 64, 64), BF16),
            pltpu.VMEM((LEVELS, 64, 64), BF16),
            pltpu.VMEM((128, 2048), BF16),
            pltpu.VMEM((4, 64, 2048), BF16),
            pltpu.VMEM((256, LEVELS * 128), BF16),
            pltpu.VMEM((LEVELS, 128, 128), BF16),
            pltpu.VMEM((8, 8, 128), F32),
            pltpu.VMEM((48, 16, 128), BF16),
            pltpu.VMEM((LEVELS - 1, 8, 128), BF16),
            pltpu.VMEM((NY * NZ, 8, 128), BF16),
            pltpu.VMEM((16, 2048), F32),
            pltpu.VMEM((4, 4, 2048), BF16),
            pltpu.VMEM((4, 4, 2048), BF16),
            pltpu.SemaphoreType.DMA((16,)),
            pltpu.SemaphoreType.DMA((12,)),
            pltpu.SemaphoreType.DMA((12,)),
            pltpu.SemaphoreType.DMA((LEVELS - 1,)),
            pltpu.SemaphoreType.REGULAR((3,)),
        ],
        compiler_params=pltpu.CompilerParams(
            collective_id=0, has_side_effects=True, vmem_limit_bytes=48 * 2**20
        ),
        name="h2_product",
    )(*(pltpu.with_memory_space_constraint(a, pltpu.HBM) for a in operands))


def solution(mesh):
    in_specs = (
        P("vec", "leaf"),
        P(("leaf", "vec"), None, None, None),
        P(("leaf", "vec"), None),
        P(("leaf", "vec"), None, None),
        P("leaf", None, None),
        P("leaf", None, None, None),
        P("leaf", None),
        P("leaf"),
        P("leaf", None, None, None),
        P("leaf", None, None, None),
    )
    return jax.shard_map(
        local, mesh=mesh, in_specs=in_specs, out_specs=P("vec", "leaf"), check_vma=False
    )
```
